256 devices in a mesh: row: 16 (over y, x), col: 16 (over z, core).
Axes of the slice: x: 4, y: 4, z: 8, core: 2. Of those that a mesh axis runs over, the one named last changes fastest.
Arguments:
- panel: float32 [32768, 512], P('row', 'col'), may hold values from -6 to 6
- trailing: float32 [32768, 8192], P('row', 'col'), may hold values from -6 to 6
Outputs:
- r_factor: float32 [512, 512], P(None, 'col')
- top_rows: float32 [512, 8192], P(None, 'col')
- projected: float32 [32768, 8192], P('row', 'col')
The draws below stay inside these ranges and needn't reach their ends.
All inputs are finite; a program needn't handle non-finite values.
Results may differ from the reference program's by a relative error of at most 0.0003.
Values sent between devices are 32-bit elements; how exact they have to be, the bound alone decides.
No kernel may reach another device: no remote copies, remote signals or barrier semaphores. Data moves between devices by JAX's collectives and lax.ppermute only.
A program may use at most 64 MiB of HBM per device.

```python
import jax
import jax.numpy as jnp
from jax import lax

NB = 512
ROWS = 32768
NT = 8192


def level_of(own_key, shape, cuts, low, high):
    loudness, own = 1.0, jax.random.fold_in(own_key, 6)
    for axis_at, shards_of in cuts:
        steps = jnp.exp(jax.random.uniform(jax.random.fold_in(own, axis_at), (shards_of,), jnp.float32, low / len(cuts), high / len(cuts)))
        loudness = loudness * jnp.repeat(steps, shape[axis_at] // shards_of).reshape([-1 if axis == axis_at else 1 for axis in range(len(shape))])
    return loudness


def noise(key, dims, deviation, bound, pieces=(), held_as=jnp.bfloat16):
    result = deviation * jax.random.normal(key, dims, jnp.float32)
    if pieces:
        result = result * level_of(key, dims, pieces, -0.22, 0.18)
    return jnp.clip(result, -bound, bound).astype(held_as)


def setup_inputs(seed: int = 0) -> dict:
    keys = jax.random.split(jax.random.key(seed), 3)
    return {
        "panel": noise(keys[0], (ROWS, NB), 1.0, 6.0, ((0, 16), (1, 16)), jnp.float32),
        "trailing": noise(keys[1], (ROWS, NT), 1.0, 6.0, ((0, 16), (1, 16)), jnp.float32),
    }


def reference(panel, trailing):
    highest = lax.Precision.HIGHEST
    basis, upper = jnp.linalg.qr(panel)
    signs = jnp.where(jnp.diagonal(upper) < 0, -1.0, 1.0).astype(panel.dtype)
    upper = upper * signs[:, None]
    basis = basis * signs[None, :]
    top_rows = jnp.dot(basis.T, trailing, precision=highest)
    projected = trailing - jnp.dot(basis, top_rows, precision=highest)
    return (upper, top_rows, projected)
```

```python
import functools

import jax
import jax.numpy as jnp
from jax import lax
from jax.experimental import pallas as pl
from jax.experimental.pallas import tpu as pltpu
from jax.sharding import PartitionSpec as P

HIGHEST = lax.Precision.HIGHEST
HIGH = lax.Precision.HIGH
BLOCK = 128
SIDE = 4


def matmul(left, right, left_dim, right_dim, precision):
    return lax.dot_general(
        left, right, (((left_dim,), (right_dim,)), ((), ())),
        precision=precision, preferred_element_type=jnp.float32,
    )


def factor_block(rows):
    count = len(rows)
    lane = lax.broadcasted_iota(jnp.int32, (8, BLOCK), 1)
    sub = lax.broadcasted_iota(jnp.int32, (8, BLOCK), 0)
    extra = [jnp.where(lane == sub + 8 * g, 1.0, 0.0).astype(jnp.float32) for g in range(count)]
    upper, inverse = [], []
    for p in range(count):
        first = 8 * p
        top, ext = rows[p], extra[p]
        cols = [jnp.broadcast_to(top[:, first + m : first + m + 1], (8, BLOCK)) for m in range(8)]
        for j in range(8):
            pivot = jnp.broadcast_to(cols[j][j : j + 1, :], (8, BLOCK))
            factor = jnp.where(sub > j, cols[j] * (1.0 / pivot), 0.0)
            for m in range(j + 1, 8):
                cols[m] = cols[m] - factor * jnp.broadcast_to(cols[m][j : j + 1, :], (8, BLOCK))
            if j < 7:
                top = top - factor * jnp.broadcast_to(top[j : j + 1, :], (8, BLOCK))
                ext = ext - factor * jnp.broadcast_to(ext[j : j + 1, :], (8, BLOCK))
        pivots = cols[0]
        for j in range(1, 8):
            pivots = jnp.where(sub == j, cols[j], pivots)
        scale = lax.rsqrt(pivots)
        top = jnp.where(lane >= sub + first, top * scale, 0.0)
        ext = ext * scale
        upper.append(top)
        inverse.append(ext)
        if p + 1 < count:
            turned = top.T
            for g in range(p + 1, count):
                for i in range(8):
                    weight = jnp.broadcast_to(turned[8 * g : 8 * g + 8, i : i + 1], (8, BLOCK))
                    rows[g] = rows[g] - weight * jnp.broadcast_to(top[i : i + 1, :], (8, BLOCK))
                    extra[g] = extra[g] - weight * jnp.broadcast_to(ext[i : i + 1, :], (8, BLOCK))
    return jnp.concatenate(upper, 0), jnp.concatenate(inverse, 0)


def eliminate(k, size, work, upper):
    start = pl.multiple_of(k * BLOCK, BLOCK)
    here = pl.ds(start, BLOCK)
    groups = [work[pl.ds(pl.multiple_of(start + 8 * g, 8), 8), here] for g in range(BLOCK // 8)]
    diag, diag_inv = factor_block(groups)
    solved = matmul(diag_inv, work[here, :], 1, 0, HIGHEST)
    lane = lax.broadcasted_iota(jnp.int32, (BLOCK, size), 1)
    upper[here, :] = jnp.where(lane >= start + BLOCK, solved, 0.0)
    work[here, :] = jnp.where(lane < start, solved, 0.0)
    work[here, here] = diag_inv

    @pl.when(k < size // BLOCK - 1)
    def _():
        weights = upper[here, :]
        change = matmul(weights, jnp.where(lane >= start + BLOCK, solved, work[here, :]), 0, 0, HIGHEST)
        row = lax.broadcasted_iota(jnp.int32, (size, size), 0)
        col = lax.broadcasted_iota(jnp.int32, (size, size), 1)
        old = work[...]
        base = jnp.where((col >= start) & (col < start + BLOCK), 0.0, old)
        work[...] = jnp.where(row >= start + BLOCK, base - change, old)

    upper[here, here] = diag


def first_kernel(steps, gram_ref, work_ref, upper_ref):
    size = work_ref.shape[0]
    count = size // BLOCK
    work_ref[...] = jnp.zeros_like(work_ref)
    upper_ref[...] = jnp.zeros_like(upper_ref)
    for g in range(count):
        here = slice(g * BLOCK, (g + 1) * BLOCK)
        for t in range(count - 1):
            j = g + t
            part = gram_ref[here, t * BLOCK : (t + 1) * BLOCK]
            if j < count:
                work_ref[here, j * BLOCK : (j + 1) * BLOCK] = part
            elif (j - count, g) == (0, count - 1):
                work_ref[0:BLOCK, here] = part.T

    def step(k, carry):
        eliminate(k, size, work_ref, upper_ref)
        return carry

    lax.fori_loop(0, steps, step, 0)


def second_kernel(begin, work_in, upper_in, work_ref, upper_ref):
    size = work_ref.shape[0]
    work_ref[...] = work_in[...]
    upper_ref[...] = upper_in[...]

    def step(k, carry):
        eliminate(k, size, work_ref, upper_ref)
        return carry

    lax.fori_loop(begin, size // BLOCK, step, 0)


def in_vmem(kernel, operands, size, name):
    vmem = pl.BlockSpec(memory_space=pltpu.VMEM)
    return pl.pallas_call(
        kernel,
        out_shape=[jax.ShapeDtypeStruct((size, size), jnp.float32)] * 2,
        in_specs=[vmem] * len(operands),
        out_specs=[vmem] * 2,
        compiler_params=pltpu.CompilerParams(vmem_limit_bytes=24 << 20),
        cost_estimate=pl.CostEstimate(flops=20_000_000_000, bytes_accessed=4 << 20, transcendentals=0),
        name=name,
    )(*operands)


def shifted(dy, dx):
    return [(y * SIDE + x, (y + dy) % SIDE * SIDE + (x + dx) % SIDE) for y in range(SIDE) for x in range(SIDE)]


def sum_along(value, along_y):
    total = value
    for k in range(1, SIDE):
        total = total + lax.ppermute(value, "row", shifted(k, 0) if along_y else shifted(0, k))
    return total


LINES = [[y * SIDE + x for x in range(SIDE)] for y in range(SIDE)]


def on_device(panel, trailing):
    own = panel.T
    width = own.shape[0] * lax.axis_size("col")
    rows_t = lax.all_gather(own, "col", axis=0, tiled=True)
    part = matmul(own, rows_t, 1, 1, HIGHEST)
    group = lax.axis_index("col") * own.shape[0] // BLOCK
    part = lax.dynamic_slice_in_dim(jnp.concatenate([part, part], 1), group * BLOCK, width - BLOCK, 1)
    part = sum_along(sum_along(part, False), True)
    gram = lax.all_gather(part, "col", axis=0, tiled=True)

    mixed = matmul(rows_t, trailing, 1, 0, HIGH)
    mixed = lax.psum_scatter(mixed, "row", scatter_dimension=0, tiled=True, axis_index_groups=LINES)
    mixed = sum_along(mixed, True)

    work, upper = in_vmem(functools.partial(first_kernel, 2), (gram,), width, "factor_first")
    mixed = lax.all_gather(mixed, "row", axis=0, tiled=True, axis_index_groups=LINES)
    inverse_t, upper = in_vmem(functools.partial(second_kernel, 2), (work, upper), width, "factor_second")

    top_rows = matmul(inverse_t, mixed, 1, 0, HIGH)
    coefs = matmul(inverse_t, top_rows, 0, 0, HIGH)
    projected = trailing - matmul(rows_t, coefs, 0, 0, HIGH)
    r_factor = lax.dynamic_slice_in_dim(upper, lax.axis_index("col") * own.shape[0], own.shape[0], 1)
    return (r_factor, top_rows, projected)


def solution(mesh):
    placed = (P("row", "col"), P("row", "col"))
    return jax.shard_map(
        on_device,
        mesh=mesh,
        in_specs=placed,
        out_specs=(P(None, "col"), P(None, "col"), P("row", "col")),
        check_vma=False,
    )
```

```python
import functools

import jax
import jax.numpy as jnp
from jax import lax
from jax.experimental import pallas as pl
from jax.experimental.pallas import tpu as pltpu
from jax.sharding import PartitionSpec as P

BLOCK = 128
SIDE = 4
NARROW = 32


def three_parts(value):
    high = value.astype(jnp.bfloat16)
    rest = value - high.astype(jnp.float32)
    middle = rest.astype(jnp.bfloat16)
    return high, middle, (rest - middle.astype(jnp.float32)).astype(jnp.bfloat16)


def exact_product(left, right, left_dim, right_dim):
    a, b = three_parts(left), three_parts(right)
    return lax.dot_general(
        jnp.concatenate([a[0], a[0], a[1], a[1], a[0], a[2]], left_dim),
        jnp.concatenate([b[0], b[1], b[0], b[1], b[2], b[0]], right_dim),
        (((left_dim,), (right_dim,)), ((), ())),
        preferred_element_type=jnp.float32,
    )


def one_row(value, j):
    return jnp.broadcast_to(value[j : j + 1, :], value.shape)


def factor_block(rows):
    count, wide, step = len(rows), 4, 2
    lane = lax.broadcasted_iota(jnp.int32, (8, BLOCK), 1)
    sub = lax.broadcasted_iota(jnp.int32, (8, BLOCK), 0)
    extra = [jnp.where(lane == sub + 8 * g, 1.0, 0.0).astype(jnp.float32) for g in range(count)]
    for p in range(0, count, wide):
        for q in range(p, p + wide, step):
            live = range(q, p + wide)
            cols = {
                g: [jnp.broadcast_to(rows[g][:, 8 * q + m : 8 * q + m + 1], (8, BLOCK)) for m in range(8 * step)]
                for g in live
            }
            pivots = {}
            for j in range(8 * step):
                group, at = q + j // 8, j % 8
                scale = 1.0 / one_row(cols[group][j], at)
                top, ext = one_row(rows[group], at), one_row(extra[group], at)
                entries = {m: one_row(cols[group][m], at) for m in range(j + 1, 8 * step)}
                for g in live:
                    if g < group:
                        continue
                    factor = cols[g][j] * scale
                    if g == group:
                        factor = jnp.where(sub > at, factor, 0.0)
                    for m in range(j + 1, 8 * step):
                        cols[g][m] = cols[g][m] - factor * entries[m]
                    rows[g] = rows[g] - factor * top
                    extra[g] = extra[g] - factor * ext
                pivots[group] = cols[group][j] if at == 0 else jnp.where(sub == at, cols[group][j], pivots[group])
            for g in range(q, q + step):
                scale = lax.rsqrt(pivots[g])
                rows[g] = jnp.where(lane >= sub + 8 * g, rows[g] * scale, 0.0)
                extra[g] = extra[g] * scale
        if p + wide < count:
            solved = jnp.concatenate(rows[p : p + wide], 0)
            both = jnp.concatenate([solved, jnp.concatenate(extra[p : p + wide], 0)], 1)
            change = exact_product(solved, both, 0, 0)
            for g in range(p + wide, count):
                rows[g] = rows[g] - change[8 * g : 8 * g + 8, :BLOCK]
                extra[g] = extra[g] - change[8 * g : 8 * g + 8, BLOCK:]
    return jnp.concatenate(rows, 0), jnp.concatenate(extra, 0)


def eliminate(begin, end, work, upper):
    size = work.shape[0]

    def step(k, carry):
        start = pl.multiple_of(k * BLOCK, BLOCK)
        groups = [work[pl.ds(pl.multiple_of(start + 8 * g, 8), 8), pl.ds(start, BLOCK)] for g in range(BLOCK // 8)]
        diag, diag_inv = factor_block(groups)
        for i in range(begin, end):

            @pl.when(k == i)
            def _(first=i * BLOCK, last=(i + 1) * BLOCK):
                here = slice(first, last)
                solved = exact_product(diag_inv, work[here, :], 1, 0)
                pieces = [diag_inv]
                if first:
                    work[here, :first] = solved[:, :first]
                    pieces = [solved[:, :first], diag_inv]
                work[here, here] = diag_inv
                upper[here, here] = diag
                if last < size:
                    right = solved[:, last:]
                    work[here, last:] = jnp.zeros_like(right)
                    upper[here, last:] = right
                    change = exact_product(right, jnp.concatenate(pieces + [right], 1), 0, 0)
                    if first:
                        work[last:, :first] = work[last:, :first] - change[:, :first]
                    work[last:, here] = -change[:, here]
                    work[last:, last:] = work[last:, last:] - change[:, last:]

        return carry

    lax.fori_loop(begin, end, step, 0)


def first_kernel(steps, part_ref, work_ref, upper_ref):
    size = work_ref.shape[0]
    chips = size // (2 * NARROW)
    upper_ref[...] = jnp.zeros_like(upper_ref)
    pair = 2 * NARROW
    tall = part_ref.shape[0] // (2 * chips)
    far = chips // 2

    def columns_of(z, c, s):
        first = (2 * z + c) * tall
        return part_ref[first : first + pair, s * NARROW : (s + 1) * NARROW]

    for z in range(chips):
        here = slice(z * pair, (z + 1) * pair)
        for s in range(far):
            lower = (z - s) % chips
            block = jnp.concatenate([columns_of(z, 0, s), columns_of(lower, 1, s)], 1)
            if lower <= z:
                work_ref[lower * pair : (lower + 1) * pair, here] = block
            else:
                work_ref[here, lower * pair : (lower + 1) * pair] = block.T
        if z >= far:
            for c in range(2):
                first = (2 * z + c) * tall + pair
                row = (2 * (z - far) + c) * NARROW
                work_ref[row : row + NARROW, here] = part_ref[first : first + NARROW, 0:pair]

    eliminate(0, steps, work_ref, upper_ref)


def second_kernel(begin, place_ref, work_in, upper_in, work_ref, upper_ref, own_ref, turned_ref):
    size = work_ref.shape[0]

    eliminate(begin, size // BLOCK, work_ref, upper_ref)
    first = place_ref[0] * NARROW
    group = pl.multiple_of(first // BLOCK * BLOCK, BLOCK)
    turned_ref[...] = upper_ref[:, pl.ds(group, BLOCK)].T
    own_ref[...] = turned_ref[pl.ds(pl.multiple_of(lax.rem(first, BLOCK), NARROW), NARROW), :]


VMEM = pl.BlockSpec(memory_space=pltpu.VMEM)
SMEM = pl.BlockSpec(memory_space=pltpu.SMEM)
HBM = pl.BlockSpec(memory_space=pltpu.HBM)


def cost(flops):
    return pl.CostEstimate(flops=flops, bytes_accessed=1 << 20, transcendentals=0)


def in_vmem(value):
    return pltpu.with_memory_space_constraint(value, pltpu.VMEM)


def scalar(value):
    return jnp.asarray(value, jnp.int32).reshape(1)


def factor_first(parts, size, steps):
    return pl.pallas_call(
        functools.partial(first_kernel, steps),
        out_shape=[jax.ShapeDtypeStruct((size, size), jnp.float32)] * 2,
        in_specs=[VMEM],
        out_specs=[VMEM] * 2,
        compiler_params=pltpu.CompilerParams(vmem_limit_bytes=16 << 20),
        cost_estimate=cost(10_000_000_000),
        name="factor_first",
    )(parts)


def factor_second(work, upper, begin):
    size = work.shape[0]
    return pl.pallas_call(
        functools.partial(second_kernel, begin),
        out_shape=[jax.ShapeDtypeStruct((size, size), jnp.float32)] * 2 + [jax.ShapeDtypeStruct((NARROW, size), jnp.float32)],
        in_specs=[SMEM, VMEM, VMEM],
        out_specs=[VMEM] * 3,
        scratch_shapes=[pltpu.VMEM((BLOCK, size), jnp.float32)],
        input_output_aliases={1: 0, 2: 1},
        compiler_params=pltpu.CompilerParams(vmem_limit_bytes=16 << 20),
        cost_estimate=cost(8_000_000_000),
        name="factor_second",
    )(scalar(lax.axis_index("col")), work, upper)


def shifted(dy, dx):
    return [(y * SIDE + x, (y + dy) % SIDE * SIDE + (x + dx) % SIDE) for y in range(SIDE) for x in range(SIDE)]


def sent_along(value, along_y):
    return [lax.ppermute(value, "row", shifted(k, 0) if along_y else shifted(0, k)) for k in range(1, SIDE)]


def sum_along(value, along_y):
    return sum(sent_along(value, along_y), value)


LINES = [[y * SIDE + x for x in range(SIDE)] for y in range(SIDE)]


def split(value):
    high = value.astype(jnp.bfloat16)
    return high, (value - high.astype(jnp.float32)).astype(jnp.bfloat16)


def three_products(left, right, left_dim, right_dim):
    def one(a, b):
        return lax.dot_general(a, b, (((left_dim,), (right_dim,)), ((), ())), preferred_element_type=jnp.float32)

    return one(left[0], right[0]) + (one(left[0], right[1]) + one(left[1], right[0]))


def part_kernel(core_ref, own_ref, other_ref, *refs):
    part_ref, own, sem = refs[-3:]
    refs = refs[:-2]
    load = pltpu.make_async_copy(own_ref, own, sem)
    load.start()
    load.wait()
    own_ref = own
    narrow = own_ref.shape[0]
    even = core_ref[0] == 0
    blocks = jnp.concatenate([own_ref[...], other_ref[...]] + [ref[...] for ref in refs[:-1]], 0)
    count, pair = blocks.shape[0], 2 * narrow
    left = three_parts(blocks)
    right = jnp.concatenate([part[:pair] for part in left], 0)
    products = lax.dot_general(
        jnp.concatenate(left, 0), right, (((1,), (1,)), ((), ())), preferred_element_type=jnp.float32
    )

    def piece(i, j):
        return products[i * count : (i + 1) * count, j * pair : (j + 1) * pair]

    total = piece(0, 0) + ((piece(0, 1) + piece(1, 0)) + (piece(1, 1) + (piece(0, 2) + piece(2, 0))))
    columns = [jnp.concatenate([jnp.where(even, total[:narrow, :narrow], total[narrow:pair, :narrow]),
                                jnp.where(even, total[narrow:pair, :narrow], total[:narrow, :narrow])], 0)]
    for first in range(pair, count - narrow, pair):
        turned = total[first : first + narrow].T
        swapped = jnp.concatenate([turned[narrow:], turned[:narrow]], 0)
        columns.append(jnp.where(even, total[first : first + pair, :narrow], swapped))
    tail = total[count - narrow :]
    tail = jnp.where(even, tail, jnp.concatenate([tail[:, narrow:], tail[:, :narrow]], 1))
    tail = jnp.concatenate([tail, jnp.zeros((narrow, (len(columns) - 2) * narrow), jnp.float32)], 1)
    part_ref[...] = jnp.concatenate([jnp.concatenate(columns, 1), tail], 0)


def gram_part(own, other, blocks):
    return pl.pallas_call(
        part_kernel,
        out_shape=jax.ShapeDtypeStruct((3 * NARROW, 4 * NARROW), jnp.float32),
        in_specs=[SMEM, HBM] + [VMEM] * (1 + len(blocks)),
        out_specs=VMEM,
        scratch_shapes=[pltpu.VMEM(own.shape, jnp.float32), pltpu.SemaphoreType.DMA],
        compiler_params=pltpu.CompilerParams(vmem_limit_bytes=16 << 20),
        cost_estimate=cost(2_000_000_000),
        name="gram_part",
    )(scalar(lax.rem(lax.axis_index("col"), 2)), pltpu.with_memory_space_constraint(own, pltpu.HBM), in_vmem(other), *[in_vmem(block) for block in blocks])


def turn_kernel(tile, *refs):
    own_ref, *blocks, high_ref, low_ref, own, high, low, sems = refs
    load = pltpu.make_async_copy(own_ref, own, sems.at[0])
    load.start()
    load.wait()
    stores = []
    for t in range(high.shape[0]):
        rows = jnp.concatenate([ref[:, t * tile : (t + 1) * tile] for ref in [own] + blocks], 0)
        here = pl.ds(t * tile, tile)
        for value, kept, out, i in zip(split(rows.T), (high, low), (high_ref, low_ref), range(2)):
            kept[t] = value
            stores.append(pltpu.make_async_copy(kept.at[t], out.at[here, :], sems.at[1 + 2 * t + i]))
            stores[-1].start()
    for store in stores:
        store.wait()


def turn(blocks, tile):
    count = sum(block.shape[0] for block in blocks)
    depth = blocks[0].shape[1]
    tiles = depth // tile
    return pl.pallas_call(
        functools.partial(turn_kernel, tile),
        out_shape=[pltpu.HBM((depth, count), jnp.bfloat16)] * 2,
        in_specs=[HBM] + [VMEM] * (len(blocks) - 1),
        out_specs=[HBM, HBM],
        scratch_shapes=[pltpu.VMEM(blocks[0].shape, jnp.float32)]
        + [pltpu.VMEM((tiles, tile, count), jnp.bfloat16)] * 2
        + [pltpu.SemaphoreType.DMA((2 * tiles + 1,))],
        compiler_params=pltpu.CompilerParams(vmem_limit_bytes=16 << 20),
        cost_estimate=cost(3_000_000_000),
        name="turn",
    )(pltpu.with_memory_space_constraint(blocks[0], pltpu.HBM), *[in_vmem(block) for block in blocks[1:]])


def mixed_kernel(tile, turned, place_ref, *refs):
    own_ref, *blocks = refs[: -(10 + SIDE)]
    trailing_ref, *quarter_refs = refs[-(10 + SIDE) : -9]
    high_ref, low_ref, own, taken, high, low, loads_sem, stores_sem, whole = refs[-9:]
    tiles = taken.shape[0]
    here = [pl.ds(t * tile, tile) for t in range(tiles)]
    load_own = pltpu.make_async_copy(own_ref, own, loads_sem.at[tiles])
    load_own.start()
    loads = [pltpu.make_async_copy(trailing_ref.at[here[t], :], taken.at[t], loads_sem.at[t]) for t in range(tiles)]
    for load in loads:
        load.start()
    load_own.wait()
    blocks = [own] + blocks
    stores = []
    for t in range(tiles):
        rows = split(jnp.concatenate([ref[:, t * tile : (t + 1) * tile] for ref in blocks], 0))
        loads[t].wait()
        product = three_products(rows, split(taken[t]), 1, 0)
        whole[...] = product if t == 0 else whole[...] + product
        for value, kept, out, i in ((rows[0], high, high_ref, 0), (rows[1], low, low_ref, 1)):
            kept[t] = value[-turned:].T
            stores.append(pltpu.make_async_copy(kept.at[t], out.at[here[t], :], stores_sem.at[2 * t + i]))
            stores[-1].start()
    size = whole.shape[0] // SIDE
    for k in range(SIDE):
        quarter_refs[k][...] = whole[pl.ds(pl.multiple_of(lax.rem(place_ref[0] + k, SIDE) * size, size), size), :]
    for store in stores:
        store.wait()


def mix(early, late, trailing, tile):
    depth, across = trailing.shape
    tiles = depth // tile
    blocks = early + late
    width = sum(block.shape[0] for block in blocks)
    turned = sum(block.shape[0] for block in late)
    return pl.pallas_call(
        functools.partial(mixed_kernel, tile, turned),
        out_shape=[jax.ShapeDtypeStruct((width // SIDE, across), jnp.float32)] * SIDE
        + [pltpu.HBM((depth, turned), jnp.bfloat16)] * 2,
        in_specs=[SMEM, HBM] + [VMEM] * (len(blocks) - 1) + [HBM],
        out_specs=[VMEM] * SIDE + [HBM, HBM],
        scratch_shapes=[
            pltpu.VMEM(blocks[0].shape, jnp.float32),
            pltpu.VMEM((tiles, tile, across), jnp.float32),
            pltpu.VMEM((tiles, tile, turned), jnp.bfloat16),
            pltpu.VMEM((tiles, tile, turned), jnp.bfloat16),
            pltpu.SemaphoreType.DMA((tiles + 1,)),
            pltpu.SemaphoreType.DMA((2 * tiles,)),
            pltpu.VMEM((width, across), jnp.float32),
        ],
        compiler_params=pltpu.CompilerParams(vmem_limit_bytes=20 << 20),
        cost_estimate=cost(5_000_000_000),
        name="mixed",
    )(
        scalar(lax.rem(lax.axis_index("row"), SIDE)),
        pltpu.with_memory_space_constraint(blocks[0], pltpu.HBM),
        *[in_vmem(block) for block in blocks[1:]],
        pltpu.with_memory_space_constraint(trailing, pltpu.HBM),
    )


def last_kernel(tile, place_ref, inverse_ref, *refs):
    pieces, refs = refs[:SIDE], refs[SIDE:]
    highs, lows, refs = refs[:2], refs[2:4], refs[4:]
    trailing_ref, top_ref, out_ref, rows, tiles, sems = refs
    width = inverse_ref.shape[0]
    count = width // NARROW
    quarter = count // SIDE

    def placed(i):
        return pl.ds(pl.multiple_of(place_ref[i] * NARROW, NARROW), NARROW)

    for k in range(SIDE):
        for j in range(quarter):
            at = placed(lax.rem(place_ref[count] - k + SIDE, SIDE) * quarter + j)
            rows[at, :] = pieces[k][j * NARROW : (j + 1) * NARROW, :]
    inverse = split(inverse_ref[...])
    top = three_products(inverse, split(rows[...]), 1, 0)
    top_ref[...] = top
    rows[...] = three_products(inverse, split(top), 0, 0)
    weights = split(jnp.concatenate([rows[placed(i), :] for i in range(count)], 0))
    copies = []
    for t in range(trailing_ref.shape[0] // tile):
        here = slice(t * tile, (t + 1) * tile)
        left = [jnp.concatenate([a[here, :], b[here, :]], 1) for a, b in (highs, lows)]
        tiles[t] = trailing_ref[here, :] - three_products(left, weights, 1, 0)
        copies.append(pltpu.make_async_copy(tiles.at[t], out_ref.at[pl.ds(t * tile, tile), :], sems.at[t]))
        copies[-1].start()
    for copy in copies:
        copy.wait()


def finish(places, inverse_t, pieces, highs, lows, trailing, tile):
    depth, across = trailing.shape
    width = inverse_t.shape[0]
    return pl.pallas_call(
        functools.partial(last_kernel, tile),
        out_shape=[
            jax.ShapeDtypeStruct((width, across), jnp.float32),
            jax.ShapeDtypeStruct((depth, across), jnp.float32),
        ],
        in_specs=[SMEM] + [VMEM] * (2 + SIDE + 2 * len(highs)),
        out_specs=[VMEM, pl.BlockSpec(memory_space=pl.ANY)],
        scratch_shapes=[pltpu.VMEM((width, across), jnp.float32)]
        + [pltpu.VMEM((depth // tile, tile, across), jnp.float32), pltpu.SemaphoreType.DMA((depth // tile,))],
        compiler_params=pltpu.CompilerParams(vmem_limit_bytes=24 << 20),
        cost_estimate=cost(8_000_000_000),
        name="finish",
    )(places, inverse_t, *pieces, *highs, *lows, trailing)


def round_z(chips):
    return [(2 * z + c, 2 * ((z + 1 - 2 * c) % chips) + c) for z in range(chips) for c in range(2)]


def on_device(panel, trailing):
    own = panel.T
    narrow = own.shape[0]
    devices = lax.axis_size("col")
    chips = devices // 2
    width = narrow * devices
    far = chips // 2
    ring = round_z(chips)
    swap = [(i, i ^ 1) for i in range(devices)]

    def send(value):
        return lax.ppermute(value, "col", ring)

    def exchange(value):
        return lax.ppermute(value, "col", swap)

    first, second = [own], [exchange(own)]
    blocks = [own, second[0]]
    for s in range(1, far):
        first.append(send(first[-1]))
        second.append(send(second[-1]))
        blocks += [first[s], second[s], exchange(second[s]), exchange(first[s])]
    first.append(send(first[-1]))
    early = blocks[: 4 * far - 4]
    high, low = turn(early, 512)
    first[far], high = lax.optimization_barrier((first[far], high))

    received = [first[s] if core == 0 else second[s] for s in range(1, far) for core in range(2)] + [first[far]]
    part = gram_part(own, second[0], received)
    pieces = sent_along(part, False)
    late = blocks[4 * far - 4 :] + [first[far], exchange(first[far])]
    late[0], pieces[0] = lax.optimization_barrier((late[0], pieces[0]))
    *quarters, late_high, late_low = mix(early, late, trailing, 512)
    part = sum(pieces, part)
    quarters[1:] = [lax.ppermute(quarter, "row", shifted(0, k + 1)) for k, quarter in enumerate(quarters[1:])]
    part, quarters[0] = lax.optimization_barrier((sum_along(part, True), quarters[0]))
    mixed = sum(quarters[1:], quarters[0])
    mixed = sum_along(mixed, True)
    parts = lax.all_gather(part, "col", axis=0, tiled=True)

    work, upper = factor_first(parts, width, 2)
    quarters = [mixed] + sent_along(mixed, False)
    inverse_t, upper, own_factor = factor_second(work, upper, 2)

    row, col = lax.axis_index("row"), lax.axis_index("col")
    z, c = lax.div(col, 2), lax.rem(col, 2)
    places = [2 * z + c, 2 * z + 1 - c]
    for s in range(1, far):
        for chip in (z + s * (2 * c - 1), z - s * (2 * c - 1)):
            chip = lax.rem(chip + chips, chips)
            places += [2 * chip + c, 2 * chip + 1 - c]
    chip = lax.rem(z + far, chips)
    places += [2 * chip + c, 2 * chip + 1 - c, lax.rem(row, SIDE)]
    places = jnp.stack(places).astype(jnp.int32)
    top_rows, projected = finish(places, inverse_t, quarters, [high, late_high], [low, late_low], trailing, 512)
    return (own_factor.T, top_rows, projected)


def solution(mesh):
    placed = (P("row", "col"), P("row", "col"))
    return jax.shard_map(
        on_device,
        mesh=mesh,
        in_specs=placed,
        out_specs=(P(None, "col"), P(None, "col"), P("row", "col")),
        check_vma=False,
    )
```

```python
import functools

import jax
import jax.numpy as jnp
from jax import lax
from jax.experimental import pallas as pl
from jax.experimental.pallas import tpu as pltpu
from jax.sharding import PartitionSpec as P

BLOCK = 128
SIDE = 4
NARROW = 32


def three_parts(value):
    high = value.astype(jnp.bfloat16)
    rest = value - high.astype(jnp.float32)
    middle = rest.astype(jnp.bfloat16)
    return high, middle, (rest - middle.astype(jnp.float32)).astype(jnp.bfloat16)


def exact_product(left, right, left_dim, right_dim):
    a, b = three_parts(left), three_parts(right)
    return lax.dot_general(
        jnp.concatenate([a[0], a[0], a[1], a[1], a[0], a[2]], left_dim),
        jnp.concatenate([b[0], b[1], b[0], b[1], b[2], b[0]], right_dim),
        (((left_dim,), (right_dim,)), ((), ())),
        preferred_element_type=jnp.float32,
    )


def one_row(value, j):
    return jnp.broadcast_to(value[j : j + 1, :], value.shape)


def factor_block(rows):
    count, wide, step = len(rows), 4, 2
    lane = lax.broadcasted_iota(jnp.int32, (8, BLOCK), 1)
    sub = lax.broadcasted_iota(jnp.int32, (8, BLOCK), 0)
    extra = [jnp.where(lane == sub + 8 * g, 1.0, 0.0).astype(jnp.float32) for g in range(count)]
    for p in range(0, count, wide):
        for q in range(p, p + wide, step):
            live = range(q, p + wide)
            cols = {
                g: [jnp.broadcast_to(rows[g][:, 8 * q + m : 8 * q + m + 1], (8, BLOCK)) for m in range(8 * step)]
                for g in live
            }
            pivots = {}
            for j in range(8 * step):
                group, at = q + j // 8, j % 8
                scale = 1.0 / one_row(cols[group][j], at)
                top, ext = one_row(rows[group], at), one_row(extra[group], at)
                entries = {m: one_row(cols[group][m], at) for m in range(j + 1, 8 * step)}
                for g in live:
                    if g < group:
                        continue
                    factor = cols[g][j] * scale
                    if g == group:
                        factor = jnp.where(sub > at, factor, 0.0)
                    for m in range(j + 1, 8 * step):
                        cols[g][m] = cols[g][m] - factor * entries[m]
                    rows[g] = rows[g] - factor * top
                    extra[g] = extra[g] - factor * ext
                pivots[group] = cols[group][j] if at == 0 else jnp.where(sub == at, cols[group][j], pivots[group])
            for g in range(q, q + step):
                scale = lax.rsqrt(pivots[g])
                rows[g] = jnp.where(lane >= sub + 8 * g, rows[g] * scale, 0.0)
                extra[g] = extra[g] * scale
        if p + wide < count:
            solved = jnp.concatenate(rows[p : p + wide], 0)
            both = jnp.concatenate([solved, jnp.concatenate(extra[p : p + wide], 0)], 1)
            change = exact_product(solved, both, 0, 0)
            for g in range(p + wide, count):
                rows[g] = rows[g] - change[8 * g : 8 * g + 8, :BLOCK]
                extra[g] = extra[g] - change[8 * g : 8 * g + 8, BLOCK:]
    return jnp.concatenate(rows, 0), jnp.concatenate(extra, 0)


def eliminate(begin, end, work, upper):
    size = work.shape[0]

    def step(k, carry):
        start = pl.multiple_of(k * BLOCK, BLOCK)
        groups = [work[pl.ds(pl.multiple_of(start + 8 * g, 8), 8), pl.ds(start, BLOCK)] for g in range(BLOCK // 8)]
        diag, diag_inv = factor_block(groups)
        for i in range(begin, end):

            @pl.when(k == i)
            def _(first=i * BLOCK, last=(i + 1) * BLOCK):
                here = slice(first, last)
                solved = exact_product(diag_inv, work[here, :], 1, 0)
                pieces = [diag_inv]
                if first:
                    work[here, :first] = solved[:, :first]
                    pieces = [solved[:, :first], diag_inv]
                work[here, here] = diag_inv
                upper[here, here] = diag
                if last < size:
                    right = solved[:, last:]
                    work[here, last:] = jnp.zeros_like(right)
                    upper[here, last:] = right
                    change = exact_product(right, jnp.concatenate(pieces + [right], 1), 0, 0)
                    if first:
                        work[last:, :first] = work[last:, :first] - change[:, :first]
                    work[last:, here] = -change[:, here]
                    work[last:, last:] = work[last:, last:] - change[:, last:]

        return carry

    lax.fori_loop(begin, end, step, 0)


def first_kernel(steps, part_ref, work_ref, upper_ref):
    size = work_ref.shape[0]
    chips = size // (2 * NARROW)
    upper_ref[...] = jnp.zeros_like(upper_ref)
    pair = 2 * NARROW
    tall = part_ref.shape[0] // (2 * chips)
    far = chips // 2

    def columns_of(z, c, s):
        first = (2 * z + c) * tall
        return part_ref[first : first + pair, s * NARROW : (s + 1) * NARROW]

    for z in range(chips):
        here = slice(z * pair, (z + 1) * pair)
        for s in range(far):
            lower = (z - s) % chips
            block = jnp.concatenate([columns_of(z, 0, s), columns_of(lower, 1, s)], 1)
            if lower <= z:
                work_ref[lower * pair : (lower + 1) * pair, here] = block
            else:
                work_ref[here, lower * pair : (lower + 1) * pair] = block.T
        if z >= far:
            for c in range(2):
                first = (2 * z + c) * tall + pair
                row = (2 * (z - far) + c) * NARROW
                work_ref[row : row + NARROW, here] = part_ref[first : first + NARROW, 0:pair]

    eliminate(0, steps, work_ref, upper_ref)


def split(value):
    high = value.astype(jnp.bfloat16)
    return high, (value - high.astype(jnp.float32)).astype(jnp.bfloat16)


def three_products(left, right, left_dim, right_dim):
    def one(a, b):
        return lax.dot_general(a, b, (((left_dim,), (right_dim,)), ((), ())), preferred_element_type=jnp.float32)

    return one(left[0], right[0]) + (one(left[0], right[1]) + one(left[1], right[0]))


def second_kernel(begin, place_ref, work_in, upper_in, work_ref, upper_ref, own_ref, *refs):
    by_piece_refs, by_block_refs, (turned_ref, inverse_ref) = refs[:2], refs[2:4], refs[4:]
    size = work_ref.shape[0]
    count = size // NARROW
    eliminate(begin, size // BLOCK, work_ref, upper_ref)
    inverse_ref[...] = work_ref[...].T

    def rows(at):
        return inverse_ref[pl.ds(pl.multiple_of(place_ref[at] * NARROW, NARROW), NARROW), :]

    near = split(jnp.concatenate([rows(i) for i in range(count)], 0))
    quarter = count // SIDE
    first = [lax.rem(place_ref[count] - k + SIDE, SIDE) * quarter for k in range(SIDE)]
    pieces = split(jnp.concatenate([rows(first[k] + j) for k in range(SIDE) for j in range(quarter)], 0).T)
    for i in range(2):
        by_block_refs[i][...] = near[i]
        by_piece_refs[i][...] = pieces[i]
    first = place_ref[0] * NARROW
    group = pl.multiple_of(first // BLOCK * BLOCK, BLOCK)
    turned_ref[...] = upper_ref[:, pl.ds(group, BLOCK)].T
    own_ref[...] = turned_ref[pl.ds(pl.multiple_of(lax.rem(first, BLOCK), NARROW), NARROW), :]


VMEM = pl.BlockSpec(memory_space=pltpu.VMEM)
SMEM = pl.BlockSpec(memory_space=pltpu.SMEM)
HBM = pl.BlockSpec(memory_space=pltpu.HBM)


def cost(flops):
    return pl.CostEstimate(flops=flops, bytes_accessed=1 << 20, transcendentals=0)


def in_vmem(value):
    return pltpu.with_memory_space_constraint(value, pltpu.VMEM)


def scalar(value):
    return jnp.asarray(value, jnp.int32).reshape(1)


def factor_first(parts, size, steps):
    return pl.pallas_call(
        functools.partial(first_kernel, steps),
        out_shape=[jax.ShapeDtypeStruct((size, size), jnp.float32)] * 2,
        in_specs=[VMEM],
        out_specs=[VMEM] * 2,
        compiler_params=pltpu.CompilerParams(vmem_limit_bytes=10 << 20),
        cost_estimate=cost(10_000_000_000),
        name="factor_first",
    )(parts)


def factor_second(places, work, upper, begin):
    size = work.shape[0]
    whole = jax.ShapeDtypeStruct((size, size), jnp.float32)
    return pl.pallas_call(
        functools.partial(second_kernel, begin),
        out_shape=[whole, whole, jax.ShapeDtypeStruct((NARROW, size), jnp.float32)]
        + [pltpu.VMEM((size, size), jnp.bfloat16)] * 4,
        in_specs=[SMEM, VMEM, VMEM],
        out_specs=[VMEM] * 7,
        scratch_shapes=[pltpu.VMEM((BLOCK, size), jnp.float32), pltpu.VMEM((size, size), jnp.float32)],
        input_output_aliases={1: 0, 2: 1},
        compiler_params=pltpu.CompilerParams(vmem_limit_bytes=12 << 20),
        cost_estimate=cost(8_000_000_000),
        name="factor_second",
    )(places, work, upper)


def shifted(dy, dx):
    return [(y * SIDE + x, (y + dy) % SIDE * SIDE + (x + dx) % SIDE) for y in range(SIDE) for x in range(SIDE)]


def sent_along(value, along_y):
    return [lax.ppermute(value, "row", shifted(k, 0) if along_y else shifted(0, k)) for k in range(1, SIDE)]


def sum_along(value, along_y):
    return sum(sent_along(value, along_y), value)


LINES = [[y * SIDE + x for x in range(SIDE)] for y in range(SIDE)]


def part_kernel(core_ref, own_ref, other_ref, *refs):
    part_ref = refs[-1]
    narrow = own_ref.shape[0]
    even = core_ref[0] == 0
    left = three_parts(jnp.concatenate([own_ref[...], other_ref[...]] + [ref[...] for ref in refs[:-1]], 0))
    count, pair = left[0].shape[0], 2 * narrow
    right = jnp.concatenate([part[:pair] for part in left], 0)
    products = lax.dot_general(
        jnp.concatenate(left, 0), right, (((1,), (1,)), ((), ())), preferred_element_type=jnp.float32
    )

    def piece(i, j):
        return products[i * count : (i + 1) * count, j * pair : (j + 1) * pair]

    total = piece(0, 0) + ((piece(0, 1) + piece(1, 0)) + (piece(1, 1) + (piece(0, 2) + piece(2, 0))))
    columns = [jnp.concatenate([jnp.where(even, total[:narrow, :narrow], total[narrow:pair, :narrow]),
                                jnp.where(even, total[narrow:pair, :narrow], total[:narrow, :narrow])], 0)]
    for first in range(pair, count - narrow, pair):
        turned = total[first : first + narrow].T
        swapped = jnp.concatenate([turned[narrow:], turned[:narrow]], 0)
        columns.append(jnp.where(even, total[first : first + pair, :narrow], swapped))
    tail = total[count - narrow :]
    tail = jnp.where(even, tail, jnp.concatenate([tail[:, narrow:], tail[:, :narrow]], 1))
    tail = jnp.concatenate([tail, jnp.zeros((narrow, (len(columns) - 2) * narrow), jnp.float32)], 1)
    part_ref[...] = jnp.concatenate([jnp.concatenate(columns, 1), tail], 0)


def gram_part(own, other, blocks):
    return pl.pallas_call(
        part_kernel,
        out_shape=jax.ShapeDtypeStruct((3 * NARROW, 4 * NARROW), jnp.float32),
        in_specs=[SMEM] + [VMEM] * (2 + len(blocks)),
        out_specs=VMEM,
        compiler_params=pltpu.CompilerParams(vmem_limit_bytes=10 << 20),
        cost_estimate=cost(2_000_000_000),
        name="gram_part",
    )(scalar(lax.rem(lax.axis_index("col"), 2)), *[in_vmem(block) for block in (own, other, *blocks)])


def products_and_turned(tile, blocks, taken, loads, trailing_into, kept, outs, sems):
    stores = []
    for t, load in enumerate(loads):
        rows = split(jnp.concatenate([ref[:, t * tile : (t + 1) * tile] for ref in blocks], 0))
        for value, turned, out, i in zip(rows, kept, outs, range(2)):
            turned[t] = value.T
            stores.append(pltpu.make_async_copy(turned.at[t], out.at[pl.ds(t * tile, tile), :], sems.at[2 * t + i]))
            stores[-1].start()
        load.wait()
        trailing_into(t, three_products(rows, split(taken[t]), 1, 0))
    return stores


def load_tiles(tile, trailing_ref, taken, sems):
    loads = [
        pltpu.make_async_copy(trailing_ref.at[pl.ds(t * tile, tile), :], taken.at[t], sems.at[t])
        for t in range(taken.shape[0])
    ]
    for load in loads:
        load.start()
    return loads


def mixed_kernel(tile, own_ref, *refs):
    *blocks, trailing_ref, mixed_ref, own, high_ref, low_ref, taken, high, low, loads_sem, stores_sem, whole = refs
    load_own = pltpu.make_async_copy(own_ref, own, loads_sem.at[taken.shape[0]])
    load_own.start()
    loads = load_tiles(tile, trailing_ref, taken, loads_sem)

    def put(t, product):
        whole[...] = product if t == 0 else whole[...] + product

    load_own.wait()
    outs = high_ref, low_ref
    stores = products_and_turned(tile, [own] + blocks, taken, loads, put, (high, low), outs, stores_sem)
    stores.append(pltpu.make_async_copy(whole, mixed_ref, loads_sem.at[0]))
    stores[-1].start()
    for store in stores:
        store.wait()


def mixed_last_kernel(tile, place_ref, done_ref, *refs):
    *blocks, trailing_ref = refs[: -(SIDE + 8)]
    quarter_refs, (high_ref, low_ref, taken, high, low, loads_sem, stores_sem, whole) = refs[-(SIDE + 8) : -8], refs[-8:]
    loads = load_tiles(tile, trailing_ref, taken, loads_sem)
    count = done_ref.shape[0]
    load_done = pltpu.make_async_copy(done_ref, whole.at[pl.ds(0, count), :], loads_sem.at[taken.shape[0]])
    load_done.start()

    def put(t, product):
        whole[count:, :] = product if t == 0 else whole[count:, :] + product

    outs = high_ref, low_ref
    stores = products_and_turned(tile, blocks, taken, loads, put, (high, low), outs, stores_sem)
    load_done.wait()
    size = whole.shape[0] // SIDE
    for k in range(SIDE):
        quarter_refs[k][...] = whole[pl.ds(pl.multiple_of(lax.rem(place_ref[0] + k, SIDE) * size, size), size), :]
    for store in stores:
        store.wait()


def scratch_for(depth, across, count, tile):
    tiles = depth // tile
    return [
        pltpu.VMEM((tiles, tile, across), jnp.float32),
        pltpu.VMEM((tiles, tile, count), jnp.bfloat16),
        pltpu.VMEM((tiles, tile, count), jnp.bfloat16),
        pltpu.SemaphoreType.DMA((tiles + 1,)),
        pltpu.SemaphoreType.DMA((2 * tiles,)),
    ]


def mix(blocks, trailing, tile):
    count = sum(block.shape[0] for block in blocks)
    depth, across = trailing.shape
    return pl.pallas_call(
        functools.partial(mixed_kernel, tile),
        out_shape=[pltpu.HBM((count, across), jnp.float32), pltpu.VMEM(blocks[0].shape, jnp.float32)]
        + [pltpu.HBM((depth, count), jnp.bfloat16)] * 2,
        in_specs=[HBM] + [VMEM] * (len(blocks) - 1) + [HBM],
        out_specs=[HBM, VMEM, HBM, HBM],
        scratch_shapes=scratch_for(depth, across, count, tile) + [pltpu.VMEM((count, across), jnp.float32)],
        compiler_params=pltpu.CompilerParams(vmem_limit_bytes=14 << 20),
        cost_estimate=cost(3_000_000_000),
        name="mixed",
    )(
        pltpu.with_memory_space_constraint(blocks[0], pltpu.HBM),
        *[in_vmem(block) for block in blocks[1:]],
        pltpu.with_memory_space_constraint(trailing, pltpu.HBM),
    )


def mix_last(done, blocks, trailing, tile):
    count = sum(block.shape[0] for block in blocks)
    depth, across = trailing.shape
    width = done.shape[0] + count
    return pl.pallas_call(
        functools.partial(mixed_last_kernel, tile),
        out_shape=[jax.ShapeDtypeStruct((width // SIDE, across), jnp.float32)] * SIDE
        + [pltpu.HBM((depth, count), jnp.bfloat16)] * 2,
        in_specs=[SMEM, HBM] + [VMEM] * len(blocks) + [HBM],
        out_specs=[VMEM] * SIDE + [HBM, HBM],
        scratch_shapes=scratch_for(depth, across, count, tile) + [pltpu.VMEM((width, across), jnp.float32)],
        compiler_params=pltpu.CompilerParams(vmem_limit_bytes=12 << 20),
        cost_estimate=cost(3_000_000_000),
        name="mixed_last",
    )(
        scalar(lax.rem(lax.axis_index("row"), SIDE)),
        pltpu.with_memory_space_constraint(done, pltpu.HBM),
        *[in_vmem(block) for block in blocks],
        pltpu.with_memory_space_constraint(trailing, pltpu.HBM),
    )


def last_kernel(tile, *refs):
    by_piece, by_block, pieces, refs = refs[:2], refs[2:4], refs[4 : 4 + SIDE], refs[4 + SIDE :]
    highs, lows, refs = refs[:2], refs[2:4], refs[4:]
    trailing_ref, top_ref, out_ref, top, tiles, sems = refs
    count = tiles.shape[0]
    values = split(jnp.concatenate([ref[...] for ref in pieces], 0))
    product = three_products([ref[...] for ref in by_piece], values, 1, 0)
    top[...] = product
    copies = [pltpu.make_async_copy(top, top_ref, sems.at[count])]
    copies[0].start()
    weights = split(three_products([ref[...] for ref in by_block], split(product), 1, 0))
    for t in range(count):
        here = slice(t * tile, (t + 1) * tile)
        left = [jnp.concatenate([a[here, :], b[here, :]], 1) for a, b in (highs, lows)]
        tiles[t] = trailing_ref[here, :] - three_products(left, weights, 1, 0)
        copies.append(pltpu.make_async_copy(tiles.at[t], out_ref.at[pl.ds(t * tile, tile), :], sems.at[t]))
        copies[-1].start()
    for copy in copies:
        copy.wait()


def finish(by_piece, by_block, pieces, highs, lows, trailing, tile):
    depth, across = trailing.shape
    width = by_block[0].shape[0]
    tiles = depth // tile
    operands = *by_piece, *by_block, *pieces, *highs, *lows, trailing
    return pl.pallas_call(
        functools.partial(last_kernel, tile),
        out_shape=[
            jax.ShapeDtypeStruct((width, across), jnp.float32),
            jax.ShapeDtypeStruct((depth, across), jnp.float32),
        ],
        in_specs=[VMEM] * len(operands),
        out_specs=[pl.BlockSpec(memory_space=pl.ANY)] * 2,
        scratch_shapes=[
            pltpu.VMEM((width, across), jnp.float32),
            pltpu.VMEM((tiles, tile, across), jnp.float32),
            pltpu.SemaphoreType.DMA((tiles + 1,)),
        ],
        compiler_params=pltpu.CompilerParams(vmem_limit_bytes=16 << 20),
        cost_estimate=cost(8_000_000_000),
        name="finish",
    )(*[in_vmem(operand) for operand in operands])


def round_z(chips):
    return [(2 * z + c, 2 * ((z + 1 - 2 * c) % chips) + c) for z in range(chips) for c in range(2)]


def on_device(panel, trailing):
    own = panel.T
    narrow = own.shape[0]
    devices = lax.axis_size("col")
    chips = devices // 2
    width = narrow * devices
    far = chips // 2
    ring = round_z(chips)
    swap = [(i, i ^ 1) for i in range(devices)]

    def send(value):
        return lax.ppermute(value, "col", ring)

    def exchange(value):
        return lax.ppermute(value, "col", swap)

    first, second = [own], [exchange(own)]
    blocks = [own, second[0]]
    for s in range(1, far):
        first.append(send(first[-1]))
        second.append(send(second[-1]))
        blocks += [first[s], second[s], exchange(second[s]), exchange(first[s])]
    first.append(send(first[-1]))
    early = blocks[: 4 * far - 4]
    mixed, near, high, low = mix(early, trailing, 512)
    first[far], mixed = lax.optimization_barrier((first[far], mixed))

    received = [first[s] if core == 0 else second[s] for s in range(1, far) for core in range(2)] + [first[far]]
    part = gram_part(near, second[0], received)
    pieces = sent_along(part, False)
    late = blocks[4 * far - 4 :] + [first[far], exchange(first[far])]
    late[0], pieces[0] = lax.optimization_barrier((late[0], pieces[0]))
    *quarters, late_high, late_low = mix_last(mixed, late, trailing, 512)
    part = sum(pieces, part)
    quarters[1:] = [lax.ppermute(quarter, "row", shifted(0, k + 1)) for k, quarter in enumerate(quarters[1:])]
    part, quarters[0] = lax.optimization_barrier((sum_along(part, True), quarters[0]))
    mixed = sum(quarters[1:], quarters[0])
    mixed = sum_along(mixed, True)
    parts = lax.all_gather(part, "col", axis=0, tiled=True)

    row, col = lax.axis_index("row"), lax.axis_index("col")
    z, c = lax.div(col, 2), lax.rem(col, 2)
    places = [2 * z + c, 2 * z + 1 - c]
    for s in range(1, far):
        for chip in (z + s * (2 * c - 1), z - s * (2 * c - 1)):
            chip = lax.rem(chip + chips, chips)
            places += [2 * chip + c, 2 * chip + 1 - c]
    chip = lax.rem(z + far, chips)
    places += [2 * chip + c, 2 * chip + 1 - c, lax.rem(row, SIDE)]
    places = jnp.stack(places).astype(jnp.int32)

    work, upper = factor_first(parts, width, 2)
    quarters = [mixed] + sent_along(mixed, False)
    _, _, own_factor, *arranged = factor_second(places, work, upper, 2)
    highs, lows = [high, late_high], [low, late_low]
    top_rows, projected = finish(arranged[:2], arranged[2:], quarters, highs, lows, trailing, 512)
    return (own_factor.T, top_rows, projected)


def solution(mesh):
    placed = (P("row", "col"), P("row", "col"))
    return jax.shard_map(
        on_device,
        mesh=mesh,
        in_specs=placed,
        out_specs=(P(None, "col"), P(None, "col"), P("row", "col")),
        check_vma=False,
    )
```

```python
import functools

import jax
import jax.numpy as jnp
from jax import lax
from jax.experimental import pallas as pl
from jax.experimental.pallas import tpu as pltpu
from jax.sharding import PartitionSpec as P

BLOCK = 128
SIDE = 4
NARROW = 32


def three_parts(value):
    high = value.astype(jnp.bfloat16)
    rest = value - high.astype(jnp.float32)
    middle = rest.astype(jnp.bfloat16)
    return high, middle, (rest - middle.astype(jnp.float32)).astype(jnp.bfloat16)


def exact_product(left, right, left_dim, right_dim):
    a, b = three_parts(left), three_parts(right)
    return lax.dot_general(
        jnp.concatenate([a[0], a[0], a[1], a[1], a[0], a[2]], left_dim),
        jnp.concatenate([b[0], b[1], b[0], b[1], b[2], b[0]], right_dim),
        (((left_dim,), (right_dim,)), ((), ())),
        preferred_element_type=jnp.float32,
    )


def one_row(value, j):
    return jnp.broadcast_to(value[j : j + 1, :], value.shape)


def factor_block(rows):
    count, wide, step = len(rows), 4, 2
    lane = lax.broadcasted_iota(jnp.int32, (8, BLOCK), 1)
    sub = lax.broadcasted_iota(jnp.int32, (8, BLOCK), 0)
    extra = [jnp.where(lane == sub + 8 * g, 1.0, 0.0).astype(jnp.float32) for g in range(count)]
    for p in range(0, count, wide):
        for q in range(p, p + wide, step):
            live = range(q, p + wide)
            cols = {
                g: [jnp.broadcast_to(rows[g][:, 8 * q + m : 8 * q + m + 1], (8, BLOCK)) for m in range(8 * step)]
                for g in live
            }
            pivots = {}
            for j in range(8 * step):
                group, at = q + j // 8, j % 8
                scale = 1.0 / one_row(cols[group][j], at)
                top, ext = one_row(rows[group], at), one_row(extra[group], at)
                entries = {m: one_row(cols[group][m], at) for m in range(j + 1, 8 * step)}
                for g in live:
                    if g < group:
                        continue
                    factor = cols[g][j] * scale
                    if g == group:
                        factor = jnp.where(sub > at, factor, 0.0)
                    for m in range(j + 1, 8 * step):
                        cols[g][m] = cols[g][m] - factor * entries[m]
                    rows[g] = rows[g] - factor * top
                    extra[g] = extra[g] - factor * ext
                pivots[group] = cols[group][j] if at == 0 else jnp.where(sub == at, cols[group][j], pivots[group])
            for g in range(q, q + step):
                scale = lax.rsqrt(pivots[g])
                rows[g] = jnp.where(lane >= sub + 8 * g, rows[g] * scale, 0.0)
                extra[g] = extra[g] * scale
        if p + wide < count:
            solved = jnp.concatenate(rows[p : p + wide], 0)
            both = jnp.concatenate([solved, jnp.concatenate(extra[p : p + wide], 0)], 1)
            change = exact_product(solved, both, 0, 0)
            for g in range(p + wide, count):
                rows[g] = rows[g] - change[8 * g : 8 * g + 8, :BLOCK]
                extra[g] = extra[g] - change[8 * g : 8 * g + 8, BLOCK:]
    return jnp.concatenate(rows, 0), jnp.concatenate(extra, 0)


def eliminate(begin, end, work, upper):
    size = work.shape[0]

    def step(k, carry):
        start = pl.multiple_of(k * BLOCK, BLOCK)
        groups = [work[pl.ds(pl.multiple_of(start + 8 * g, 8), 8), pl.ds(start, BLOCK)] for g in range(BLOCK // 8)]
        diag, diag_inv = factor_block(groups)
        for i in range(begin, end):

            @pl.when(k == i)
            def _(first=i * BLOCK, last=(i + 1) * BLOCK):
                here = slice(first, last)
                solved = exact_product(diag_inv, work[here, :], 1, 0)
                pieces = [diag_inv]
                if first:
                    work[here, :first] = solved[:, :first]
                    pieces = [solved[:, :first], diag_inv]
                work[here, here] = diag_inv
                upper[here, here] = diag
                if last < size:
                    right = solved[:, last:]
                    work[here, last:] = jnp.zeros_like(right)
                    upper[here, last:] = right
                    change = exact_product(right, jnp.concatenate(pieces + [right], 1), 0, 0)
                    if first:
                        work[last:, :first] = work[last:, :first] - change[:, :first]
                    work[last:, here] = -change[:, here]
                    work[last:, last:] = work[last:, last:] - change[:, last:]

        return carry

    lax.fori_loop(begin, end, step, 0)


def first_kernel(steps, part_ref, work_ref, upper_ref):
    size = work_ref.shape[0]
    chips = size // (2 * NARROW)
    upper_ref[...] = jnp.zeros_like(upper_ref)
    pair = 2 * NARROW
    tall = part_ref.shape[0] // (2 * chips)
    far = chips // 2

    def columns_of(z, c, s):
        first = (2 * z + c) * tall
        return part_ref[first : first + pair, s * NARROW : (s + 1) * NARROW]

    for z in range(chips):
        here = slice(z * pair, (z + 1) * pair)
        for s in range(far):
            lower = (z - s) % chips
            block = jnp.concatenate([columns_of(z, 0, s), columns_of(lower, 1, s)], 1)
            if lower <= z:
                work_ref[lower * pair : (lower + 1) * pair, here] = block
            else:
                work_ref[here, lower * pair : (lower + 1) * pair] = block.T
        if z >= far:
            for c in range(2):
                first = (2 * z + c) * tall + pair
                row = (2 * (z - far) + c) * NARROW
                work_ref[row : row + NARROW, here] = part_ref[first : first + NARROW, 0:pair]

    eliminate(0, steps, work_ref, upper_ref)


def split(value):
    high = value.astype(jnp.bfloat16)
    return high, (value - high.astype(jnp.float32)).astype(jnp.bfloat16)


def three_products(left, right, left_dim, right_dim):
    def one(a, b):
        return lax.dot_general(a, b, (((left_dim,), (right_dim,)), ((), ())), preferred_element_type=jnp.float32)

    return one(left[0], right[0]) + (one(left[0], right[1]) + one(left[1], right[0]))


def second_kernel(begin, place_ref, work_in, upper_in, work_ref, upper_ref, own_ref, *refs):
    by_piece_refs, by_block_refs, (turned_ref, inverse_ref) = refs[:2], refs[2:4], refs[4:]
    size = work_ref.shape[0]
    count = size // NARROW
    eliminate(begin, size // BLOCK, work_ref, upper_ref)
    inverse_ref[...] = work_ref[...].T

    def rows(at):
        return inverse_ref[pl.ds(pl.multiple_of(place_ref[at] * NARROW, NARROW), NARROW), :]

    near = split(jnp.concatenate([rows(i) for i in range(count)], 0))
    quarter = count // SIDE
    first = [lax.rem(place_ref[count] - k + SIDE, SIDE) * quarter for k in range(SIDE)]
    pieces = split(jnp.concatenate([rows(first[k] + j) for k in range(SIDE) for j in range(quarter)], 0).T)
    for i in range(2):
        by_block_refs[i][...] = near[i]
        by_piece_refs[i][...] = pieces[i]
    first = place_ref[0] * NARROW
    group = pl.multiple_of(first // BLOCK * BLOCK, BLOCK)
    turned_ref[...] = upper_ref[:, pl.ds(group, BLOCK)].T
    own_ref[...] = turned_ref[pl.ds(pl.multiple_of(lax.rem(first, BLOCK), NARROW), NARROW), :]


VMEM = pl.BlockSpec(memory_space=pltpu.VMEM)
SMEM = pl.BlockSpec(memory_space=pltpu.SMEM)
HBM = pl.BlockSpec(memory_space=pltpu.HBM)


def cost(flops):
    return pl.CostEstimate(flops=flops, bytes_accessed=1 << 20, transcendentals=0)


def in_vmem(value):
    return pltpu.with_memory_space_constraint(value, pltpu.VMEM)


def scalar(value):
    return jnp.asarray(value, jnp.int32).reshape(1)


def factor_first(parts, size, steps):
    return pl.pallas_call(
        functools.partial(first_kernel, steps),
        out_shape=[jax.ShapeDtypeStruct((size, size), jnp.float32)] * 2,
        in_specs=[VMEM],
        out_specs=[VMEM] * 2,
        compiler_params=pltpu.CompilerParams(vmem_limit_bytes=10 << 20),
        cost_estimate=cost(10_000_000_000),
        name="factor_first",
    )(parts)


def factor_second(places, work, upper, begin):
    size = work.shape[0]
    whole = jax.ShapeDtypeStruct((size, size), jnp.float32)
    return pl.pallas_call(
        functools.partial(second_kernel, begin),
        out_shape=[whole, whole, jax.ShapeDtypeStruct((NARROW, size), jnp.float32)]
        + [pltpu.VMEM((size, size), jnp.bfloat16)] * 4,
        in_specs=[SMEM, VMEM, VMEM],
        out_specs=[VMEM] * 7,
        scratch_shapes=[pltpu.VMEM((BLOCK, size), jnp.float32), pltpu.VMEM((size, size), jnp.float32)],
        input_output_aliases={1: 0, 2: 1},
        compiler_params=pltpu.CompilerParams(vmem_limit_bytes=12 << 20),
        cost_estimate=cost(8_000_000_000),
        name="factor_second",
    )(places, work, upper)


def shifted(dy, dx):
    return [(y * SIDE + x, (y + dy) % SIDE * SIDE + (x + dx) % SIDE) for y in range(SIDE) for x in range(SIDE)]


def sent_along(value, along_y):
    return [lax.ppermute(value, "row", shifted(k, 0) if along_y else shifted(0, k)) for k in range(1, SIDE)]


def sum_along(value, along_y):
    return sum(sent_along(value, along_y), value)


LINES = [[y * SIDE + x for x in range(SIDE)] for y in range(SIDE)]


def part_kernel(core_ref, own_ref, other_ref, *refs):
    part_ref = refs[-1]
    narrow = own_ref.shape[0]
    even = core_ref[0] == 0
    left = three_parts(jnp.concatenate([own_ref[...], other_ref[...]] + [ref[...] for ref in refs[:-1]], 0))
    count, pair = left[0].shape[0], 2 * narrow
    right = jnp.concatenate([part[:pair] for part in left], 0)
    products = lax.dot_general(
        jnp.concatenate(left, 0), right, (((1,), (1,)), ((), ())), preferred_element_type=jnp.float32
    )

    def piece(i, j):
        return products[i * count : (i + 1) * count, j * pair : (j + 1) * pair]

    total = piece(0, 0) + ((piece(0, 1) + piece(1, 0)) + (piece(1, 1) + (piece(0, 2) + piece(2, 0))))
    columns = [jnp.concatenate([jnp.where(even, total[:narrow, :narrow], total[narrow:pair, :narrow]),
                                jnp.where(even, total[narrow:pair, :narrow], total[:narrow, :narrow])], 0)]
    for first in range(pair, count - narrow, pair):
        turned = total[first : first + narrow].T
        swapped = jnp.concatenate([turned[narrow:], turned[:narrow]], 0)
        columns.append(jnp.where(even, total[first : first + pair, :narrow], swapped))
    tail = total[count - narrow :]
    tail = jnp.where(even, tail, jnp.concatenate([tail[:, narrow:], tail[:, :narrow]], 1))
    tail = jnp.concatenate([tail, jnp.zeros((narrow, (len(columns) - 2) * narrow), jnp.float32)], 1)
    part_ref[...] = jnp.concatenate([jnp.concatenate(columns, 1), tail], 0)


def gram_part(own, other, blocks):
    return pl.pallas_call(
        part_kernel,
        out_shape=jax.ShapeDtypeStruct((3 * NARROW, 4 * NARROW), jnp.float32),
        in_specs=[SMEM] + [VMEM] * (2 + len(blocks)),
        out_specs=VMEM,
        compiler_params=pltpu.CompilerParams(vmem_limit_bytes=10 << 20),
        cost_estimate=cost(2_000_000_000),
        name="gram_part",
    )(scalar(lax.rem(lax.axis_index("col"), 2)), *[in_vmem(block) for block in (own, other, *blocks)])


def products_and_turned(tile, blocks, taken, loads, trailing_into, kept, outs, sems):
    stores = []
    for t, load in enumerate(loads):
        rows = split(jnp.concatenate([ref[:, t * tile : (t + 1) * tile] for ref in blocks], 0))
        for value, turned, out, i in zip(rows, kept, outs, range(2)):
            turned[t] = value.T
            stores.append(pltpu.make_async_copy(turned.at[t], out.at[pl.ds(t * tile, tile), :], sems.at[2 * t + i]))
            stores[-1].start()
        load.wait()
        trailing_into(t, three_products(rows, split(taken[t]), 1, 0))
    return stores


def load_tiles(tile, trailing_ref, taken, sems):
    loads = [
        pltpu.make_async_copy(trailing_ref.at[pl.ds(t * tile, tile), :], taken.at[t], sems.at[t])
        for t in range(taken.shape[0])
    ]
    for load in loads:
        load.start()
    return loads


def mixed_kernel(tile, own_ref, *refs):
    *blocks, trailing_ref, mixed_ref, own, high_ref, low_ref, taken, high, low, loads_sem, stores_sem, whole = refs
    load_own = pltpu.make_async_copy(own_ref, own, loads_sem.at[taken.shape[0]])
    load_own.start()
    loads = load_tiles(tile, trailing_ref, taken, loads_sem)

    def put(t, product):
        whole[...] = product if t == 0 else whole[...] + product

    load_own.wait()
    outs = high_ref, low_ref
    stores = products_and_turned(tile, [own] + blocks, taken, loads, put, (high, low), outs, stores_sem)
    stores.append(pltpu.make_async_copy(whole, mixed_ref, loads_sem.at[0]))
    stores[-1].start()
    for store in stores:
        store.wait()


def mixed_last_kernel(tile, place_ref, done_ref, *refs):
    *blocks, trailing_ref = refs[: -(SIDE + 8)]
    quarter_refs, (high_ref, low_ref, taken, high, low, loads_sem, stores_sem, whole) = refs[-(SIDE + 8) : -8], refs[-8:]
    loads = load_tiles(tile, trailing_ref, taken, loads_sem)
    count = done_ref.shape[0]
    load_done = pltpu.make_async_copy(done_ref, whole.at[pl.ds(0, count), :], loads_sem.at[taken.shape[0]])
    load_done.start()

    def put(t, product):
        whole[count:, :] = product if t == 0 else whole[count:, :] + product

    outs = high_ref, low_ref
    stores = products_and_turned(tile, blocks, taken, loads, put, (high, low), outs, stores_sem)
    load_done.wait()
    size = whole.shape[0] // SIDE
    for k in range(SIDE):
        quarter_refs[k][...] = whole[pl.ds(pl.multiple_of(lax.rem(place_ref[0] + k, SIDE) * size, size), size), :]
    for store in stores:
        store.wait()


def scratch_for(depth, across, count, tile):
    tiles = depth // tile
    return [
        pltpu.VMEM((tiles, tile, across), jnp.float32),
        pltpu.VMEM((tiles, tile, count), jnp.bfloat16),
        pltpu.VMEM((tiles, tile, count), jnp.bfloat16),
        pltpu.SemaphoreType.DMA((tiles + 1,)),
        pltpu.SemaphoreType.DMA((2 * tiles,)),
    ]


def mix(blocks, trailing, tile):
    count = sum(block.shape[0] for block in blocks)
    depth, across = trailing.shape
    return pl.pallas_call(
        functools.partial(mixed_kernel, tile),
        out_shape=[pltpu.HBM((count, across), jnp.float32), pltpu.VMEM(blocks[0].shape, jnp.float32)]
        + [pltpu.HBM((depth, count), jnp.bfloat16)] * 2,
        in_specs=[HBM] + [VMEM] * (len(blocks) - 1) + [HBM],
        out_specs=[HBM, VMEM, HBM, HBM],
        scratch_shapes=scratch_for(depth, across, count, tile) + [pltpu.VMEM((count, across), jnp.float32)],
        compiler_params=pltpu.CompilerParams(vmem_limit_bytes=14 << 20),
        cost_estimate=cost(3_000_000_000),
        name="mixed",
    )(
        pltpu.with_memory_space_constraint(blocks[0], pltpu.HBM),
        *[in_vmem(block) for block in blocks[1:]],
        pltpu.with_memory_space_constraint(trailing, pltpu.HBM),
    )


def mix_last(done, blocks, trailing, tile):
    count = sum(block.shape[0] for block in blocks)
    depth, across = trailing.shape
    width = done.shape[0] + count
    return pl.pallas_call(
        functools.partial(mixed_last_kernel, tile),
        out_shape=[jax.ShapeDtypeStruct((width // SIDE, across), jnp.float32)] * SIDE
        + [pltpu.HBM((depth, count), jnp.bfloat16)] * 2,
        in_specs=[SMEM, HBM] + [VMEM] * len(blocks) + [HBM],
        out_specs=[VMEM] * SIDE + [HBM, HBM],
        scratch_shapes=scratch_for(depth, across, count, tile) + [pltpu.VMEM((width, across), jnp.float32)],
        compiler_params=pltpu.CompilerParams(vmem_limit_bytes=12 << 20),
        cost_estimate=cost(3_000_000_000),
        name="mixed_last",
    )(
        scalar(lax.rem(lax.axis_index("row"), SIDE)),
        pltpu.with_memory_space_constraint(done, pltpu.HBM),
        *[in_vmem(block) for block in blocks],
        pltpu.with_memory_space_constraint(trailing, pltpu.HBM),
    )


def last_kernel(tile, *refs):
    by_piece, by_block, pieces, refs = refs[:2], refs[2:4], refs[4 : 4 + SIDE], refs[4 + SIDE :]
    highs, lows, refs = refs[:2], refs[2:4], refs[4:]
    trailing_ref, top_ref, out_ref, top, tiles, sems = refs
    count = tiles.shape[0]
    values = split(jnp.concatenate([ref[...] for ref in pieces], 0))
    product = three_products([ref[...] for ref in by_piece], values, 1, 0)
    top[...] = product
    copies = [pltpu.make_async_copy(top, top_ref, sems.at[count])]
    copies[0].start()
    weights = split(three_products([ref[...] for ref in by_block], split(product), 1, 0))
    for t in range(count):
        here = slice(t * tile, (t + 1) * tile)
        left = [jnp.concatenate([a[here, :], b[here, :]], 1) for a, b in (highs, lows)]
        tiles[t] = trailing_ref[here, :] - three_products(left, weights, 1, 0)
        copies.append(pltpu.make_async_copy(tiles.at[t], out_ref.at[pl.ds(t * tile, tile), :], sems.at[t]))
        copies[-1].start()
    for copy in copies:
        copy.wait()


def finish(by_piece, by_block, pieces, highs, lows, trailing, tile):
    depth, across = trailing.shape
    width = by_block[0].shape[0]
    tiles = depth // tile
    operands = *by_piece, *by_block, *pieces, *highs, *lows, trailing
    return pl.pallas_call(
        functools.partial(last_kernel, tile),
        out_shape=[
            jax.ShapeDtypeStruct((width, across), jnp.float32),
            jax.ShapeDtypeStruct((depth, across), jnp.float32),
        ],
        in_specs=[VMEM] * len(operands),
        out_specs=[pl.BlockSpec(memory_space=pl.ANY)] * 2,
        scratch_shapes=[
            pltpu.VMEM((width, across), jnp.float32),
            pltpu.VMEM((tiles, tile, across), jnp.float32),
            pltpu.SemaphoreType.DMA((tiles + 1,)),
        ],
        compiler_params=pltpu.CompilerParams(vmem_limit_bytes=16 << 20),
        cost_estimate=cost(8_000_000_000),
        name="finish",
    )(*[in_vmem(operand) for operand in operands])


def round_z(chips):
    return [(2 * z + c, 2 * ((z + 1 - 2 * c) % chips) + c) for z in range(chips) for c in range(2)]


def on_device(panel, trailing):
    own = panel.T
    narrow = own.shape[0]
    devices = lax.axis_size("col")
    chips = devices // 2
    width = narrow * devices
    far = chips // 2
    ring = round_z(chips)
    swap = [(i, i ^ 1) for i in range(devices)]

    def send(value):
        return lax.ppermute(value, "col", ring)

    def exchange(value):
        return lax.ppermute(value, "col", swap)

    first, second = [own], [exchange(own)]
    blocks = [own, second[0]]
    for s in range(1, far):
        first.append(send(first[-1]))
        second.append(send(second[-1]))
        blocks += [first[s], second[s], exchange(second[s]), exchange(first[s])]
    first.append(send(first[-1]))
    early = blocks[: 4 * far - 4]
    mixed, near, high, low = mix(early, trailing, 512)
    first[far], mixed = lax.optimization_barrier((first[far], mixed))

    received = [first[s] if core == 0 else second[s] for s in range(1, far) for core in range(2)] + [first[far]]
    part = gram_part(near, second[0], received)
    pieces = sent_along(part, False)
    late = blocks[4 * far - 4 :] + [first[far], exchange(first[far])]
    late[0], part = lax.optimization_barrier((late[0], part))
    *quarters, late_high, late_low = mix_last(mixed, late, trailing, 512)
    *pieces, quarters[0] = lax.optimization_barrier((*pieces, quarters[0]))
    part = sum(pieces, part)
    quarters[1:] = [lax.ppermute(quarter, "row", shifted(0, k + 1)) for k, quarter in enumerate(quarters[1:])]
    part, quarters[0] = lax.optimization_barrier((sum_along(part, True), quarters[0]))
    mixed = sum(quarters[1:], quarters[0])
    mixed = sum_along(mixed, True)
    parts = lax.all_gather(part, "col", axis=0, tiled=True)

    row, col = lax.axis_index("row"), lax.axis_index("col")
    z, c = lax.div(col, 2), lax.rem(col, 2)
    places = [2 * z + c, 2 * z + 1 - c]
    for s in range(1, far):
        for chip in (z + s * (2 * c - 1), z - s * (2 * c - 1)):
            chip = lax.rem(chip + chips, chips)
            places += [2 * chip + c, 2 * chip + 1 - c]
    chip = lax.rem(z + far, chips)
    places += [2 * chip + c, 2 * chip + 1 - c, lax.rem(row, SIDE)]
    places = jnp.stack(places).astype(jnp.int32)

    work, upper = factor_first(parts, width, 2)
    quarters = [mixed] + sent_along(mixed, False)
    _, _, own_factor, *arranged = factor_second(places, work, upper, 2)
    highs, lows = [high, late_high], [low, late_low]
    top_rows, projected = finish(arranged[:2], arranged[2:], quarters, highs, lows, trailing, 512)
    return (own_factor.T, top_rows, projected)


def solution(mesh):
    placed = (P("row", "col"), P("row", "col"))
    return jax.shard_map(
        on_device,
        mesh=mesh,
        in_specs=placed,
        out_specs=(P(None, "col"), P(None, "col"), P("row", "col")),
        check_vma=False,
    )
```

```python
import functools

import jax
import jax.numpy as jnp
from jax import lax
from jax.experimental import pallas as pl
from jax.experimental.pallas import tpu as pltpu
from jax.sharding import PartitionSpec as P

BLOCK = 128
SIDE = 4
STEPS = 1, 2, 3
LARGE_STEPS = 3, 1, 2
NARROW = 32


def three_parts(value):
    high = value.astype(jnp.bfloat16)
    rest = value - high.astype(jnp.float32)
    middle = rest.astype(jnp.bfloat16)
    return high, middle, (rest - middle.astype(jnp.float32)).astype(jnp.bfloat16)


def exact_product(left, right, left_dim, right_dim):
    a, b = three_parts(left), three_parts(right)
    return lax.dot_general(
        jnp.concatenate([a[0], a[0], a[1], a[1], a[0], a[2]], left_dim),
        jnp.concatenate([b[0], b[1], b[0], b[1], b[2], b[0]], right_dim),
        (((left_dim,), (right_dim,)), ((), ())),
        preferred_element_type=jnp.float32,
    )


def one_row(value, j):
    return jnp.broadcast_to(value[j : j + 1, :], value.shape)


def factor_block(rows):
    count, wide, step = len(rows), 4, 2
    lane = lax.broadcasted_iota(jnp.int32, (8, BLOCK), 1)
    sub = lax.broadcasted_iota(jnp.int32, (8, BLOCK), 0)
    extra = [jnp.where(lane == sub + 8 * g, 1.0, 0.0).astype(jnp.float32) for g in range(count)]
    for p in range(0, count, wide):
        for q in range(p, p + wide, step):
            live = range(q, p + wide)
            cols = {
                g: [jnp.broadcast_to(rows[g][:, 8 * q + m : 8 * q + m + 1], (8, BLOCK)) for m in range(8 * step)]
                for g in live
            }
            pivots = {}
            for j in range(8 * step):
                group, at = q + j // 8, j % 8
                scale = 1.0 / one_row(cols[group][j], at)
                top, ext = one_row(rows[group], at), one_row(extra[group], at)
                entries = {m: one_row(cols[group][m], at) for m in range(j + 1, 8 * step)}
                for g in live:
                    if g < group:
                        continue
                    factor = cols[g][j] * scale
                    if g == group:
                        factor = jnp.where(sub > at, factor, 0.0)
                    for m in range(j + 1, 8 * step):
                        cols[g][m] = cols[g][m] - factor * entries[m]
                    rows[g] = rows[g] - factor * top
                    extra[g] = extra[g] - factor * ext
                pivots[group] = cols[group][j] if at == 0 else jnp.where(sub == at, cols[group][j], pivots[group])
            for g in range(q, q + step):
                scale = lax.rsqrt(pivots[g])
                rows[g] = jnp.where(lane >= sub + 8 * g, rows[g] * scale, 0.0)
                extra[g] = extra[g] * scale
        if p + wide < count:
            solved = jnp.concatenate(rows[p : p + wide], 0)
            both = jnp.concatenate([solved, jnp.concatenate(extra[p : p + wide], 0)], 1)
            change = exact_product(solved, both, 0, 0)
            for g in range(p + wide, count):
                rows[g] = rows[g] - change[8 * g : 8 * g + 8, :BLOCK]
                extra[g] = extra[g] - change[8 * g : 8 * g + 8, BLOCK:]
    return jnp.concatenate(rows, 0), jnp.concatenate(extra, 0)


def eliminate(begin, end, work, upper):
    size = work.shape[0]

    def step(k, carry):
        start = pl.multiple_of(k * BLOCK, BLOCK)
        groups = [work[pl.ds(pl.multiple_of(start + 8 * g, 8), 8), pl.ds(start, BLOCK)] for g in range(BLOCK // 8)]
        diag, diag_inv = factor_block(groups)
        for i in range(begin, end):

            @pl.when(k == i)
            def _(first=i * BLOCK, last=(i + 1) * BLOCK):
                here = slice(first, last)
                solved = exact_product(diag_inv, work[here, :], 1, 0)
                pieces = [diag_inv]
                if first:
                    work[here, :first] = solved[:, :first]
                    pieces = [solved[:, :first], diag_inv]
                work[here, here] = diag_inv
                upper[here, here] = diag
                if last < size:
                    right = solved[:, last:]
                    work[here, last:] = jnp.zeros_like(right)
                    upper[here, last:] = right
                    change = exact_product(right, jnp.concatenate(pieces + [right], 1), 0, 0)
                    if first:
                        work[last:, :first] = work[last:, :first] - change[:, :first]
                    work[last:, here] = -change[:, here]
                    work[last:, last:] = work[last:, last:] - change[:, last:]

        return carry

    lax.fori_loop(begin, end, step, 0)


def first_kernel(steps, part_ref, work_ref, upper_ref):
    size = work_ref.shape[0]
    chips = size // (2 * NARROW)
    upper_ref[...] = jnp.zeros_like(upper_ref)
    pair = 2 * NARROW
    tall = part_ref.shape[0] // (2 * chips)
    far = chips // 2

    def columns_of(z, c, s):
        first = (2 * z + c) * tall
        return part_ref[first : first + pair, s * NARROW : (s + 1) * NARROW]

    for z in range(chips):
        here = slice(z * pair, (z + 1) * pair)
        for s in range(far):
            lower = (z - s) % chips
            block = jnp.concatenate([columns_of(z, 0, s), columns_of(lower, 1, s)], 1)
            if lower <= z:
                work_ref[lower * pair : (lower + 1) * pair, here] = block
            else:
                work_ref[here, lower * pair : (lower + 1) * pair] = block.T
        if z >= far:
            for c in range(2):
                first = (2 * z + c) * tall + pair
                row = (2 * (z - far) + c) * NARROW
                work_ref[row : row + NARROW, here] = part_ref[first : first + NARROW, 0:pair]

    eliminate(0, steps, work_ref, upper_ref)


def split(value):
    high = value.astype(jnp.bfloat16)
    return high, (value - high.astype(jnp.float32)).astype(jnp.bfloat16)


def three_products(left, right, left_dim, right_dim):
    def one(a, b):
        return lax.dot_general(a, b, (((left_dim,), (right_dim,)), ((), ())), preferred_element_type=jnp.float32)

    return one(left[0], right[0]) + (one(left[0], right[1]) + one(left[1], right[0]))


def second_kernel(begin, place_ref, work_in, upper_in, work_ref, upper_ref, own_ref, *refs):
    by_piece_refs, by_block_refs, (turned_ref, inverse_ref) = refs[:2], refs[2:4], refs[4:]
    size = work_ref.shape[0]
    count = size // NARROW
    eliminate(begin, size // BLOCK, work_ref, upper_ref)
    inverse_ref[...] = work_ref[...].T

    def rows(at):
        return inverse_ref[pl.ds(pl.multiple_of(place_ref[at] * NARROW, NARROW), NARROW), :]

    near = split(jnp.concatenate([rows(i) for i in range(count)], 0))
    quarter = count // SIDE
    first = [lax.rem(place_ref[count] - k + SIDE, SIDE) * quarter for k in (0, *LARGE_STEPS)]
    pieces = split(jnp.concatenate([rows(first[k] + j) for k in range(SIDE) for j in range(quarter)], 0).T)
    for i in range(2):
        by_block_refs[i][...] = near[i]
        by_piece_refs[i][...] = pieces[i]
    first = place_ref[0] * NARROW
    group = pl.multiple_of(first // BLOCK * BLOCK, BLOCK)
    turned_ref[...] = upper_ref[:, pl.ds(group, BLOCK)].T
    own_ref[...] = turned_ref[pl.ds(pl.multiple_of(lax.rem(first, BLOCK), NARROW), NARROW), :]


VMEM = pl.BlockSpec(memory_space=pltpu.VMEM)
SMEM = pl.BlockSpec(memory_space=pltpu.SMEM)
HBM = pl.BlockSpec(memory_space=pltpu.HBM)


def cost(flops):
    return pl.CostEstimate(flops=flops, bytes_accessed=1 << 20, transcendentals=0)


def in_vmem(value):
    return pltpu.with_memory_space_constraint(value, pltpu.VMEM)


def scalar(value):
    return jnp.asarray(value, jnp.int32).reshape(1)


def factor_first(parts, size, steps):
    return pl.pallas_call(
        functools.partial(first_kernel, steps),
        out_shape=[jax.ShapeDtypeStruct((size, size), jnp.float32)] * 2,
        in_specs=[VMEM],
        out_specs=[VMEM] * 2,
        compiler_params=pltpu.CompilerParams(vmem_limit_bytes=10 << 20),
        cost_estimate=cost(10_000_000_000),
        name="factor_first",
    )(parts)


def factor_second(places, work, upper, begin):
    size = work.shape[0]
    whole = jax.ShapeDtypeStruct((size, size), jnp.float32)
    return pl.pallas_call(
        functools.partial(second_kernel, begin),
        out_shape=[whole, whole, jax.ShapeDtypeStruct((NARROW, size), jnp.float32)]
        + [pltpu.VMEM((size, size), jnp.bfloat16)] * 4,
        in_specs=[SMEM, VMEM, VMEM],
        out_specs=[VMEM] * 7,
        scratch_shapes=[pltpu.VMEM((BLOCK, size), jnp.float32), pltpu.VMEM((size, size), jnp.float32)],
        input_output_aliases={1: 0, 2: 1},
        compiler_params=pltpu.CompilerParams(vmem_limit_bytes=12 << 20),
        cost_estimate=cost(8_000_000_000),
        name="factor_second",
    )(places, work, upper)


def shifted(dy, dx):
    return [(y * SIDE + x, (y + dy) % SIDE * SIDE + (x + dx) % SIDE) for y in range(SIDE) for x in range(SIDE)]


def sent_along(value, along_y, steps):
    return [lax.ppermute(value, "row", shifted(k, 0) if along_y else shifted(0, k)) for k in steps]


def sum_along(value, along_y, steps):
    return sum(sent_along(value, along_y, steps), value)


LINES = [[y * SIDE + x for x in range(SIDE)] for y in range(SIDE)]


def part_kernel(core_ref, own_ref, other_ref, *refs):
    part_ref = refs[-1]
    narrow = own_ref.shape[0]
    even = core_ref[0] == 0
    left = three_parts(jnp.concatenate([own_ref[...], other_ref[...]] + [ref[...] for ref in refs[:-1]], 0))
    count, pair = left[0].shape[0], 2 * narrow
    right = jnp.concatenate([part[:pair] for part in left], 0)
    products = lax.dot_general(
        jnp.concatenate(left, 0), right, (((1,), (1,)), ((), ())), preferred_element_type=jnp.float32
    )

    def piece(i, j):
        return products[i * count : (i + 1) * count, j * pair : (j + 1) * pair]

    total = piece(0, 0) + ((piece(0, 1) + piece(1, 0)) + (piece(1, 1) + (piece(0, 2) + piece(2, 0))))
    columns = [jnp.concatenate([jnp.where(even, total[:narrow, :narrow], total[narrow:pair, :narrow]),
                                jnp.where(even, total[narrow:pair, :narrow], total[:narrow, :narrow])], 0)]
    for first in range(pair, count - narrow, pair):
        turned = total[first : first + narrow].T
        swapped = jnp.concatenate([turned[narrow:], turned[:narrow]], 0)
        columns.append(jnp.where(even, total[first : first + pair, :narrow], swapped))
    tail = total[count - narrow :]
    tail = jnp.where(even, tail, jnp.concatenate([tail[:, narrow:], tail[:, :narrow]], 1))
    tail = jnp.concatenate([tail, jnp.zeros((narrow, (len(columns) - 2) * narrow), jnp.float32)], 1)
    part_ref[...] = jnp.concatenate([jnp.concatenate(columns, 1), tail], 0)


def gram_part(own, other, blocks):
    return pl.pallas_call(
        part_kernel,
        out_shape=jax.ShapeDtypeStruct((3 * NARROW, 4 * NARROW), jnp.float32),
        in_specs=[SMEM] + [VMEM] * (2 + len(blocks)),
        out_specs=VMEM,
        compiler_params=pltpu.CompilerParams(vmem_limit_bytes=10 << 20),
        cost_estimate=cost(2_000_000_000),
        name="gram_part",
    )(scalar(lax.rem(lax.axis_index("col"), 2)), *[in_vmem(block) for block in (own, other, *blocks)])


def products_and_turned(tile, blocks, taken, loads, trailing_into, kept, outs, sems):
    stores = []
    for t, load in enumerate(loads):
        rows = split(jnp.concatenate([ref[:, t * tile : (t + 1) * tile] for ref in blocks], 0))
        for value, turned, out, i in zip(rows, kept, outs, range(2)):
            turned[t] = value.T
            stores.append(pltpu.make_async_copy(turned.at[t], out.at[pl.ds(t * tile, tile), :], sems.at[2 * t + i]))
            stores[-1].start()
        load.wait()
        trailing_into(t, three_products(rows, split(taken[t]), 1, 0))
    return stores


def load_tiles(tile, trailing_ref, taken, sems):
    loads = [
        pltpu.make_async_copy(trailing_ref.at[pl.ds(t * tile, tile), :], taken.at[t], sems.at[t])
        for t in range(taken.shape[0])
    ]
    for load in loads:
        load.start()
    return loads


def mixed_kernel(tile, own_ref, *refs):
    *blocks, trailing_ref, mixed_ref, own, high_ref, low_ref, taken, high, low, loads_sem, stores_sem, whole = refs
    load_own = pltpu.make_async_copy(own_ref, own, loads_sem.at[taken.shape[0]])
    load_own.start()
    loads = load_tiles(tile, trailing_ref, taken, loads_sem)

    def put(t, product):
        whole[...] = product if t == 0 else whole[...] + product

    load_own.wait()
    outs = high_ref, low_ref
    stores = products_and_turned(tile, [own] + blocks, taken, loads, put, (high, low), outs, stores_sem)
    stores.append(pltpu.make_async_copy(whole, mixed_ref, loads_sem.at[0]))
    stores[-1].start()
    for store in stores:
        store.wait()


def mixed_last_kernel(tile, place_ref, done_ref, *refs):
    *blocks, trailing_ref = refs[: -(SIDE + 8)]
    quarter_refs, (high_ref, low_ref, taken, high, low, loads_sem, stores_sem, whole) = refs[-(SIDE + 8) : -8], refs[-8:]
    loads = load_tiles(tile, trailing_ref, taken, loads_sem)
    count = done_ref.shape[0]
    load_done = pltpu.make_async_copy(done_ref, whole.at[pl.ds(0, count), :], loads_sem.at[taken.shape[0]])
    load_done.start()

    def put(t, product):
        whole[count:, :] = product if t == 0 else whole[count:, :] + product

    outs = high_ref, low_ref
    stores = products_and_turned(tile, blocks, taken, loads, put, (high, low), outs, stores_sem)
    load_done.wait()
    size = whole.shape[0] // SIDE
    for k in range(SIDE):
        quarter_refs[k][...] = whole[pl.ds(pl.multiple_of(lax.rem(place_ref[0] + k, SIDE) * size, size), size), :]
    for store in stores:
        store.wait()


def scratch_for(depth, across, count, tile):
    tiles = depth // tile
    return [
        pltpu.VMEM((tiles, tile, across), jnp.float32),
        pltpu.VMEM((tiles, tile, count), jnp.bfloat16),
        pltpu.VMEM((tiles, tile, count), jnp.bfloat16),
        pltpu.SemaphoreType.DMA((tiles + 1,)),
        pltpu.SemaphoreType.DMA((2 * tiles,)),
    ]


def mix(blocks, trailing, tile):
    count = sum(block.shape[0] for block in blocks)
    depth, across = trailing.shape
    return pl.pallas_call(
        functools.partial(mixed_kernel, tile),
        out_shape=[pltpu.HBM((count, across), jnp.float32), pltpu.VMEM(blocks[0].shape, jnp.float32)]
        + [pltpu.HBM((depth, count), jnp.bfloat16)] * 2,
        in_specs=[HBM] + [VMEM] * (len(blocks) - 1) + [HBM],
        out_specs=[HBM, VMEM, HBM, HBM],
        scratch_shapes=scratch_for(depth, across, count, tile) + [pltpu.VMEM((count, across), jnp.float32)],
        compiler_params=pltpu.CompilerParams(vmem_limit_bytes=14 << 20),
        cost_estimate=cost(3_000_000_000),
        name="mixed",
    )(
        pltpu.with_memory_space_constraint(blocks[0], pltpu.HBM),
        *[in_vmem(block) for block in blocks[1:]],
        pltpu.with_memory_space_constraint(trailing, pltpu.HBM),
    )


def mix_last(done, blocks, trailing, tile):
    count = sum(block.shape[0] for block in blocks)
    depth, across = trailing.shape
    width = done.shape[0] + count
    return pl.pallas_call(
        functools.partial(mixed_last_kernel, tile),
        out_shape=[jax.ShapeDtypeStruct((width // SIDE, across), jnp.float32)] * SIDE
        + [pltpu.HBM((depth, count), jnp.bfloat16)] * 2,
        in_specs=[SMEM, HBM] + [VMEM] * len(blocks) + [HBM],
        out_specs=[VMEM] * SIDE + [HBM, HBM],
        scratch_shapes=scratch_for(depth, across, count, tile) + [pltpu.VMEM((width, across), jnp.float32)],
        compiler_params=pltpu.CompilerParams(vmem_limit_bytes=12 << 20),
        cost_estimate=cost(3_000_000_000),
        name="mixed_last",
    )(
        scalar(lax.rem(lax.axis_index("row"), SIDE)),
        pltpu.with_memory_space_constraint(done, pltpu.HBM),
        *[in_vmem(block) for block in blocks],
        pltpu.with_memory_space_constraint(trailing, pltpu.HBM),
    )


def last_kernel(tile, *refs):
    by_piece, by_block, pieces, refs = refs[:2], refs[2:4], refs[4 : 4 + SIDE], refs[4 + SIDE :]
    highs, lows, refs = refs[:2], refs[2:4], refs[4:]
    trailing_ref, top_ref, out_ref, top, tiles, sems = refs
    count = tiles.shape[0]
    values = split(jnp.concatenate([ref[...] for ref in pieces], 0))
    product = three_products([ref[...] for ref in by_piece], values, 1, 0)
    top[...] = product
    copies = [pltpu.make_async_copy(top, top_ref, sems.at[count])]
    copies[0].start()
    weights = split(three_products([ref[...] for ref in by_block], split(product), 1, 0))
    for t in range(count):
        here = slice(t * tile, (t + 1) * tile)
        left = [jnp.concatenate([a[here, :], b[here, :]], 1) for a, b in (highs, lows)]
        tiles[t] = trailing_ref[here, :] - three_products(left, weights, 1, 0)
        copies.append(pltpu.make_async_copy(tiles.at[t], out_ref.at[pl.ds(t * tile, tile), :], sems.at[t]))
        copies[-1].start()
    for copy in copies:
        copy.wait()


def finish(by_piece, by_block, pieces, highs, lows, trailing, tile):
    depth, across = trailing.shape
    width = by_block[0].shape[0]
    tiles = depth // tile
    operands = *by_piece, *by_block, *pieces, *highs, *lows, trailing
    return pl.pallas_call(
        functools.partial(last_kernel, tile),
        out_shape=[
            jax.ShapeDtypeStruct((width, across), jnp.float32),
            jax.ShapeDtypeStruct((depth, across), jnp.float32),
        ],
        in_specs=[VMEM] * len(operands),
        out_specs=[pl.BlockSpec(memory_space=pl.ANY)] * 2,
        scratch_shapes=[
            pltpu.VMEM((width, across), jnp.float32),
            pltpu.VMEM((tiles, tile, across), jnp.float32),
            pltpu.SemaphoreType.DMA((tiles + 1,)),
        ],
        compiler_params=pltpu.CompilerParams(vmem_limit_bytes=16 << 20),
        cost_estimate=cost(8_000_000_000),
        name="finish",
    )(*[in_vmem(operand) for operand in operands])


def round_z(chips):
    return [(2 * z + c, 2 * ((z + 1 - 2 * c) % chips) + c) for z in range(chips) for c in range(2)]


def on_device(panel, trailing):
    own = panel.T
    narrow = own.shape[0]
    devices = lax.axis_size("col")
    chips = devices // 2
    width = narrow * devices
    far = chips // 2
    ring = round_z(chips)
    swap = [(i, i ^ 1) for i in range(devices)]

    def send(value):
        return lax.ppermute(value, "col", ring)

    def exchange(value):
        return lax.ppermute(value, "col", swap)

    first, second = [own], [exchange(own)]
    blocks = [own, second[0]]
    for s in range(1, far):
        first.append(send(first[-1]))
        second.append(send(second[-1]))
        blocks += [first[s], second[s], exchange(second[s]), exchange(first[s])]
    first.append(send(first[-1]))
    early = blocks[: 4 * far - 4]
    mixed, near, high, low = mix(early, trailing, 512)
    first[far], mixed = lax.optimization_barrier((first[far], mixed))

    received = [first[s] if core == 0 else second[s] for s in range(1, far) for core in range(2)] + [first[far]]
    part = gram_part(near, second[0], received)
    pieces = sent_along(part, False, STEPS)
    late = blocks[4 * far - 4 :] + [first[far], exchange(first[far])]
    late[0], part = lax.optimization_barrier((late[0], part))
    *quarters, late_high, late_low = mix_last(mixed, late, trailing, 512)
    *pieces, quarters[0] = lax.optimization_barrier((*pieces, quarters[0]))
    part = sum(pieces, part)
    quarters[1:] = [lax.ppermute(quarter, "row", shifted(0, k + 1)) for k, quarter in enumerate(quarters[1:])]
    part, quarters[0] = lax.optimization_barrier((sum_along(part, True, STEPS), quarters[0]))
    mixed = sum(quarters[1:], quarters[0])
    mixed = sum_along(mixed, True, LARGE_STEPS)
    parts = lax.all_gather(part, "col", axis=0, tiled=True)

    row, col = lax.axis_index("row"), lax.axis_index("col")
    z, c = lax.div(col, 2), lax.rem(col, 2)
    places = [2 * z + c, 2 * z + 1 - c]
    for s in range(1, far):
        for chip in (z + s * (2 * c - 1), z - s * (2 * c - 1)):
            chip = lax.rem(chip + chips, chips)
            places += [2 * chip + c, 2 * chip + 1 - c]
    chip = lax.rem(z + far, chips)
    places += [2 * chip + c, 2 * chip + 1 - c, lax.rem(row, SIDE)]
    places = jnp.stack(places).astype(jnp.int32)

    work, upper = factor_first(parts, width, 2)
    quarters = [mixed] + sent_along(mixed, False, LARGE_STEPS)
    _, _, own_factor, *arranged = factor_second(places, work, upper, 2)
    highs, lows = [high, late_high], [low, late_low]
    top_rows, projected = finish(arranged[:2], arranged[2:], quarters, highs, lows, trailing, 512)
    return (own_factor.T, top_rows, projected)


def solution(mesh):
    placed = (P("row", "col"), P("row", "col"))
    return jax.shard_map(
        on_device,
        mesh=mesh,
        in_specs=placed,
        out_specs=(P(None, "col"), P(None, "col"), P("row", "col")),
        check_vma=False,
    )
```

```python
import functools

import jax
import jax.numpy as jnp
from jax import lax
from jax.experimental import pallas as pl
from jax.experimental.pallas import tpu as pltpu
from jax.sharding import PartitionSpec as P

BLOCK = 128
SIDE = 4
STEPS = 1, 2, 3
LARGE_STEPS = 3, 1, 2
NARROW = 32


def three_parts(value):
    high = value.astype(jnp.bfloat16)
    rest = value - high.astype(jnp.float32)
    middle = rest.astype(jnp.bfloat16)
    return high, middle, (rest - middle.astype(jnp.float32)).astype(jnp.bfloat16)


def exact_product(left, right, left_dim, right_dim):
    a, b = three_parts(left), three_parts(right)
    return lax.dot_general(
        jnp.concatenate([a[0], a[0], a[1], a[1], a[0], a[2]], left_dim),
        jnp.concatenate([b[0], b[1], b[0], b[1], b[2], b[0]], right_dim),
        (((left_dim,), (right_dim,)), ((), ())),
        preferred_element_type=jnp.float32,
    )


def one_row(value, j):
    return jnp.broadcast_to(value[j : j + 1, :], value.shape)


def factor_block(rows):
    count, wide, step = len(rows), 4, 2
    lane = lax.broadcasted_iota(jnp.int32, (8, BLOCK), 1)
    sub = lax.broadcasted_iota(jnp.int32, (8, BLOCK), 0)
    extra = [jnp.where(lane == sub + 8 * g, 1.0, 0.0).astype(jnp.float32) for g in range(count)]
    for p in range(0, count, wide):
        for q in range(p, p + wide, step):
            live = range(q, p + wide)
            cols = {
                g: [jnp.broadcast_to(rows[g][:, 8 * q + m : 8 * q + m + 1], (8, BLOCK)) for m in range(8 * step)]
                for g in live
            }
            pivots = {}
            for j in range(8 * step):
                group, at = q + j // 8, j % 8
                scale = 1.0 / one_row(cols[group][j], at)
                top, ext = one_row(rows[group], at), one_row(extra[group], at)
                entries = {m: one_row(cols[group][m], at) for m in range(j + 1, 8 * step)}
                for g in live:
                    if g < group:
                        continue
                    factor = cols[g][j] * scale
                    if g == group:
                        factor = jnp.where(sub > at, factor, 0.0)
                    for m in range(j + 1, 8 * step):
                        cols[g][m] = cols[g][m] - factor * entries[m]
                    rows[g] = rows[g] - factor * top
                    extra[g] = extra[g] - factor * ext
                pivots[group] = cols[group][j] if at == 0 else jnp.where(sub == at, cols[group][j], pivots[group])
            for g in range(q, q + step):
                scale = lax.rsqrt(pivots[g])
                rows[g] = jnp.where(lane >= sub + 8 * g, rows[g] * scale, 0.0)
                extra[g] = extra[g] * scale
        if p + wide < count:
            solved = jnp.concatenate(rows[p : p + wide], 0)
            both = jnp.concatenate([solved, jnp.concatenate(extra[p : p + wide], 0)], 1)
            change = exact_product(solved, both, 0, 0)
            for g in range(p + wide, count):
                rows[g] = rows[g] - change[8 * g : 8 * g + 8, :BLOCK]
                extra[g] = extra[g] - change[8 * g : 8 * g + 8, BLOCK:]
    return jnp.concatenate(rows, 0), jnp.concatenate(extra, 0)


def eliminate(begin, end, work, upper):
    size = work.shape[0]

    def step(k, carry):
        start = pl.multiple_of(k * BLOCK, BLOCK)
        groups = [work[pl.ds(pl.multiple_of(start + 8 * g, 8), 8), pl.ds(start, BLOCK)] for g in range(BLOCK // 8)]
        diag, diag_inv = factor_block(groups)
        for i in range(begin, end):

            @pl.when(k == i)
            def _(first=i * BLOCK, last=(i + 1) * BLOCK):
                here = slice(first, last)
                solved = exact_product(diag_inv, work[here, :], 1, 0)
                pieces = [diag_inv]
                if first:
                    work[here, :first] = solved[:, :first]
                    pieces = [solved[:, :first], diag_inv]
                work[here, here] = diag_inv
                upper[here, here] = diag
                if last < size:
                    right = solved[:, last:]
                    work[here, last:] = jnp.zeros_like(right)
                    upper[here, last:] = right
                    change = exact_product(right, jnp.concatenate(pieces + [right], 1), 0, 0)
                    if first:
                        work[last:, :first] = work[last:, :first] - change[:, :first]
                    work[last:, here] = -change[:, here]
                    work[last:, last:] = work[last:, last:] - change[:, last:]

        return carry

    lax.fori_loop(begin, end, step, 0)


def first_kernel(steps, part_ref, work_ref, upper_ref):
    size = work_ref.shape[0]
    chips = size // (2 * NARROW)
    upper_ref[...] = jnp.zeros_like(upper_ref)
    pair = 2 * NARROW
    tall = part_ref.shape[0] // (2 * chips)
    far = chips // 2

    def columns_of(z, c, s):
        first = (2 * z + c) * tall
        return part_ref[first : first + pair, s * NARROW : (s + 1) * NARROW]

    for z in range(chips):
        here = slice(z * pair, (z + 1) * pair)
        for s in range(far):
            lower = (z - s) % chips
            block = jnp.concatenate([columns_of(z, 0, s), columns_of(lower, 1, s)], 1)
            if lower <= z:
                work_ref[lower * pair : (lower + 1) * pair, here] = block
            else:
                work_ref[here, lower * pair : (lower + 1) * pair] = block.T
        if z >= far:
            for c in range(2):
                first = (2 * z + c) * tall + pair
                row = (2 * (z - far) + c) * NARROW
                work_ref[row : row + NARROW, here] = part_ref[first : first + NARROW, 0:pair]

    eliminate(0, steps, work_ref, upper_ref)


def split(value):
    high = value.astype(jnp.bfloat16)
    return high, (value - high.astype(jnp.float32)).astype(jnp.bfloat16)


def three_products(left, right, left_dim, right_dim):
    def one(a, b):
        return lax.dot_general(a, b, (((left_dim,), (right_dim,)), ((), ())), preferred_element_type=jnp.float32)

    return one(left[0], right[0]) + (one(left[0], right[1]) + one(left[1], right[0]))


def second_kernel(begin, place_ref, work_in, upper_in, work_ref, upper_ref, own_ref, *refs):
    by_piece_refs, by_block_refs, (turned_ref, inverse_ref) = refs[:2], refs[2:4], refs[4:]
    size = work_ref.shape[0]
    count = size // NARROW
    eliminate(begin, size // BLOCK, work_ref, upper_ref)
    inverse_ref[...] = work_ref[...].T

    def rows(at):
        return inverse_ref[pl.ds(pl.multiple_of(place_ref[at] * NARROW, NARROW), NARROW), :]

    near = split(jnp.concatenate([rows(i) for i in range(count)], 0))
    quarter = count // SIDE
    first = [lax.rem(place_ref[count] - k + SIDE, SIDE) * quarter for k in (0, *LARGE_STEPS)]
    pieces = split(jnp.concatenate([rows(first[k] + j) for k in range(SIDE) for j in range(quarter)], 0).T)
    for i in range(2):
        by_block_refs[i][...] = near[i]
        by_piece_refs[i][...] = pieces[i]
    first = place_ref[0] * NARROW
    group = pl.multiple_of(first // BLOCK * BLOCK, BLOCK)
    turned_ref[...] = upper_ref[:, pl.ds(group, BLOCK)].T
    own_ref[...] = turned_ref[pl.ds(pl.multiple_of(lax.rem(first, BLOCK), NARROW), NARROW), :]


VMEM = pl.BlockSpec(memory_space=pltpu.VMEM)
SMEM = pl.BlockSpec(memory_space=pltpu.SMEM)
HBM = pl.BlockSpec(memory_space=pltpu.HBM)


def cost(flops):
    return pl.CostEstimate(flops=flops, bytes_accessed=1 << 20, transcendentals=0)


def in_vmem(value):
    return pltpu.with_memory_space_constraint(value, pltpu.VMEM)


def scalar(value):
    return jnp.asarray(value, jnp.int32).reshape(1)


def factor_first(parts, size, steps):
    return pl.pallas_call(
        functools.partial(first_kernel, steps),
        out_shape=[jax.ShapeDtypeStruct((size, size), jnp.float32)] * 2,
        in_specs=[VMEM],
        out_specs=[VMEM] * 2,
        compiler_params=pltpu.CompilerParams(vmem_limit_bytes=10 << 20),
        cost_estimate=cost(10_000_000_000),
        name="factor_first",
    )(parts)


def factor_second(places, work, upper, begin):
    size = work.shape[0]
    whole = jax.ShapeDtypeStruct((size, size), jnp.float32)
    return pl.pallas_call(
        functools.partial(second_kernel, begin),
        out_shape=[whole, whole, jax.ShapeDtypeStruct((NARROW, size), jnp.float32)]
        + [pltpu.VMEM((size, size), jnp.bfloat16)] * 4,
        in_specs=[SMEM, VMEM, VMEM],
        out_specs=[VMEM] * 7,
        scratch_shapes=[pltpu.VMEM((BLOCK, size), jnp.float32), pltpu.VMEM((size, size), jnp.float32)],
        input_output_aliases={1: 0, 2: 1},
        compiler_params=pltpu.CompilerParams(vmem_limit_bytes=12 << 20),
        cost_estimate=cost(8_000_000_000),
        name="factor_second",
    )(places, work, upper)


def shifted(dy, dx):
    return [(y * SIDE + x, (y + dy) % SIDE * SIDE + (x + dx) % SIDE) for y in range(SIDE) for x in range(SIDE)]


def sent_along(value, along_y, steps):
    return [lax.ppermute(value, "row", shifted(k, 0) if along_y else shifted(0, k)) for k in steps]


def sum_along(value, along_y, steps):
    return sum(sent_along(value, along_y, steps), value)


LINES = [[y * SIDE + x for x in range(SIDE)] for y in range(SIDE)]


def part_kernel(core_ref, own_ref, other_ref, *refs):
    part_ref = refs[-1]
    narrow = own_ref.shape[0]
    even = core_ref[0] == 0
    left = three_parts(jnp.concatenate([own_ref[...], other_ref[...]] + [ref[...] for ref in refs[:-1]], 0))
    count, pair = left[0].shape[0], 2 * narrow
    right = jnp.concatenate([part[:pair] for part in left], 0)
    products = lax.dot_general(
        jnp.concatenate(left, 0), right, (((1,), (1,)), ((), ())), preferred_element_type=jnp.float32
    )

    def piece(i, j):
        return products[i * count : (i + 1) * count, j * pair : (j + 1) * pair]

    total = piece(0, 0) + ((piece(0, 1) + piece(1, 0)) + (piece(1, 1) + (piece(0, 2) + piece(2, 0))))
    columns = [jnp.concatenate([jnp.where(even, total[:narrow, :narrow], total[narrow:pair, :narrow]),
                                jnp.where(even, total[narrow:pair, :narrow], total[:narrow, :narrow])], 0)]
    for first in range(pair, count - narrow, pair):
        turned = total[first : first + narrow].T
        swapped = jnp.concatenate([turned[narrow:], turned[:narrow]], 0)
        columns.append(jnp.where(even, total[first : first + pair, :narrow], swapped))
    tail = total[count - narrow :]
    tail = jnp.where(even, tail, jnp.concatenate([tail[:, narrow:], tail[:, :narrow]], 1))
    tail = jnp.concatenate([tail, jnp.zeros((narrow, (len(columns) - 2) * narrow), jnp.float32)], 1)
    part_ref[...] = jnp.concatenate([jnp.concatenate(columns, 1), tail], 0)


def gram_part(own, other, blocks):
    return pl.pallas_call(
        part_kernel,
        out_shape=jax.ShapeDtypeStruct((3 * NARROW, 4 * NARROW), jnp.float32),
        in_specs=[SMEM] + [VMEM] * (2 + len(blocks)),
        out_specs=VMEM,
        compiler_params=pltpu.CompilerParams(vmem_limit_bytes=10 << 20),
        cost_estimate=cost(2_000_000_000),
        name="gram_part",
    )(scalar(lax.rem(lax.axis_index("col"), 2)), *[in_vmem(block) for block in (own, other, *blocks)])


def products_and_turned(tile, blocks, taken, loads, trailing_into, kept, outs, sems):
    stores = []
    for t, load in enumerate(loads):
        rows = split(jnp.concatenate([ref[:, t * tile : (t + 1) * tile] for ref in blocks], 0))
        for value, turned, out, i in zip(rows, kept, outs, range(2)):
            turned[t] = value.T
            stores.append(pltpu.make_async_copy(turned.at[t], out.at[pl.ds(t * tile, tile), :], sems.at[2 * t + i]))
            stores[-1].start()
        load.wait()
        trailing_into(t, three_products(rows, split(taken[t]), 1, 0))
    return stores


def load_tiles(tile, trailing_ref, taken, sems):
    loads = [
        pltpu.make_async_copy(trailing_ref.at[pl.ds(t * tile, tile), :], taken.at[t], sems.at[t])
        for t in range(taken.shape[0])
    ]
    for load in loads:
        load.start()
    return loads


def mixed_kernel(tile, own_ref, *refs):
    *blocks, trailing_ref, mixed_ref, own, high_ref, low_ref, taken, high, low, loads_sem, stores_sem, whole = refs
    load_own = pltpu.make_async_copy(own_ref, own, loads_sem.at[taken.shape[0]])
    load_own.start()
    loads = load_tiles(tile, trailing_ref, taken, loads_sem)

    def put(t, product):
        whole[...] = product if t == 0 else whole[...] + product

    load_own.wait()
    outs = high_ref, low_ref
    stores = products_and_turned(tile, [own] + blocks, taken, loads, put, (high, low), outs, stores_sem)
    stores.append(pltpu.make_async_copy(whole, mixed_ref, loads_sem.at[0]))
    stores[-1].start()
    for store in stores:
        store.wait()


def mixed_last_kernel(tile, place_ref, done_ref, *refs):
    *blocks, trailing_ref = refs[: -(SIDE + 8)]
    quarter_refs, (high_ref, low_ref, taken, high, low, loads_sem, stores_sem, whole) = refs[-(SIDE + 8) : -8], refs[-8:]
    loads = load_tiles(tile, trailing_ref, taken, loads_sem)
    count = done_ref.shape[0]
    load_done = pltpu.make_async_copy(done_ref, whole.at[pl.ds(0, count), :], loads_sem.at[taken.shape[0]])
    load_done.start()

    def put(t, product):
        whole[count:, :] = product if t == 0 else whole[count:, :] + product

    outs = high_ref, low_ref
    stores = products_and_turned(tile, blocks, taken, loads, put, (high, low), outs, stores_sem)
    load_done.wait()
    size = whole.shape[0] // SIDE
    for k in range(SIDE):
        quarter_refs[k][...] = whole[pl.ds(pl.multiple_of(lax.rem(place_ref[0] + k, SIDE) * size, size), size), :]
    for store in stores:
        store.wait()


def scratch_for(depth, across, count, tile):
    tiles = depth // tile
    return [
        pltpu.VMEM((tiles, tile, across), jnp.float32),
        pltpu.VMEM((tiles, tile, count), jnp.bfloat16),
        pltpu.VMEM((tiles, tile, count), jnp.bfloat16),
        pltpu.SemaphoreType.DMA((tiles + 1,)),
        pltpu.SemaphoreType.DMA((2 * tiles,)),
    ]


def mix(blocks, trailing, tile):
    count = sum(block.shape[0] for block in blocks)
    depth, across = trailing.shape
    return pl.pallas_call(
        functools.partial(mixed_kernel, tile),
        out_shape=[pltpu.HBM((count, across), jnp.float32), pltpu.VMEM(blocks[0].shape, jnp.float32)]
        + [pltpu.HBM((depth, count), jnp.bfloat16)] * 2,
        in_specs=[HBM] + [VMEM] * (len(blocks) - 1) + [HBM],
        out_specs=[HBM, VMEM, HBM, HBM],
        scratch_shapes=scratch_for(depth, across, count, tile) + [pltpu.VMEM((count, across), jnp.float32)],
        compiler_params=pltpu.CompilerParams(vmem_limit_bytes=14 << 20),
        cost_estimate=cost(3_000_000_000),
        name="mixed",
    )(
        pltpu.with_memory_space_constraint(blocks[0], pltpu.HBM),
        *[in_vmem(block) for block in blocks[1:]],
        pltpu.with_memory_space_constraint(trailing, pltpu.HBM),
    )


def mix_last(done, blocks, trailing, tile):
    count = sum(block.shape[0] for block in blocks)
    depth, across = trailing.shape
    width = done.shape[0] + count
    return pl.pallas_call(
        functools.partial(mixed_last_kernel, tile),
        out_shape=[jax.ShapeDtypeStruct((width // SIDE, across), jnp.float32)] * SIDE
        + [pltpu.HBM((depth, count), jnp.bfloat16)] * 2,
        in_specs=[SMEM, HBM] + [VMEM] * len(blocks) + [HBM],
        out_specs=[VMEM] * SIDE + [HBM, HBM],
        scratch_shapes=scratch_for(depth, across, count, tile) + [pltpu.VMEM((width, across), jnp.float32)],
        compiler_params=pltpu.CompilerParams(vmem_limit_bytes=12 << 20),
        cost_estimate=cost(3_000_000_000),
        name="mixed_last",
    )(
        scalar(lax.rem(lax.axis_index("row"), SIDE)),
        pltpu.with_memory_space_constraint(done, pltpu.HBM),
        *[in_vmem(block) for block in blocks],
        pltpu.with_memory_space_constraint(trailing, pltpu.HBM),
    )


def last_kernel(tile, *refs):
    by_piece, by_block, pieces, refs = refs[:2], refs[2:4], refs[4 : 4 + SIDE], refs[4 + SIDE :]
    highs, lows, refs = refs[:2], refs[2:4], refs[4:]
    trailing_ref, top_ref, out_ref, top, tiles, sems = refs
    count = tiles.shape[0]
    values = split(jnp.concatenate([ref[...] for ref in pieces], 0))
    product = three_products([ref[...] for ref in by_piece], values, 1, 0)
    top[...] = product
    copies = [pltpu.make_async_copy(top, top_ref, sems.at[count])]
    copies[0].start()
    weights = split(three_products([ref[...] for ref in by_block], split(product), 1, 0))
    for t in range(count):
        here = slice(t * tile, (t + 1) * tile)
        left = [jnp.concatenate([a[here, :], b[here, :]], 1) for a, b in (highs, lows)]
        tiles[t] = trailing_ref[here, :] - three_products(left, weights, 1, 0)
        copies.append(pltpu.make_async_copy(tiles.at[t], out_ref.at[pl.ds(t * tile, tile), :], sems.at[t]))
        copies[-1].start()
    for copy in copies:
        copy.wait()


def finish(by_piece, by_block, pieces, highs, lows, trailing, tile):
    depth, across = trailing.shape
    width = by_block[0].shape[0]
    tiles = depth // tile
    operands = *by_piece, *by_block, *pieces, *highs, *lows, trailing
    return pl.pallas_call(
        functools.partial(last_kernel, tile),
        out_shape=[
            jax.ShapeDtypeStruct((width, across), jnp.float32),
            jax.ShapeDtypeStruct((depth, across), jnp.float32),
        ],
        in_specs=[VMEM] * len(operands),
        out_specs=[pl.BlockSpec(memory_space=pl.ANY)] * 2,
        scratch_shapes=[
            pltpu.VMEM((width, across), jnp.float32),
            pltpu.VMEM((tiles, tile, across), jnp.float32),
            pltpu.SemaphoreType.DMA((tiles + 1,)),
        ],
        compiler_params=pltpu.CompilerParams(vmem_limit_bytes=16 << 20),
        cost_estimate=cost(8_000_000_000),
        name="finish",
    )(*[in_vmem(operand) for operand in operands])


def round_z(chips):
    return [(2 * z + c, 2 * ((z + 1 - 2 * c) % chips) + c) for z in range(chips) for c in range(2)]


def on_device(panel, trailing):
    own = panel.T
    narrow = own.shape[0]
    devices = lax.axis_size("col")
    chips = devices // 2
    width = narrow * devices
    far = chips // 2
    ring = round_z(chips)
    swap = [(i, i ^ 1) for i in range(devices)]

    def send(value):
        return lax.ppermute(value, "col", ring)

    def exchange(value):
        return lax.ppermute(value, "col", swap)

    first, second = [own], [exchange(own)]
    blocks = [own, second[0]]
    for s in range(1, far):
        first.append(send(first[-1]))
        second.append(send(second[-1]))
        blocks += [first[s], second[s], exchange(second[s]), exchange(first[s])]
    first.append(send(first[-1]))
    early = blocks[: 2 * far]
    mixed, near, high, low = mix(early, trailing, 512)
    first[far], mixed = lax.optimization_barrier((first[far], mixed))

    received = [first[s] if core == 0 else second[s] for s in range(1, far) for core in range(2)] + [first[far]]
    part = gram_part(near, second[0], received)
    pieces = sent_along(part, False, STEPS)
    last, part = lax.optimization_barrier((first[far], part))
    late = blocks[2 * far :] + [last, exchange(last)]
    *quarters, late_high, late_low = mix_last(mixed, late, trailing, 512)
    *pieces, quarters[0] = lax.optimization_barrier((*pieces, quarters[0]))
    part = sum(pieces, part)
    quarters[1:] = [lax.ppermute(quarter, "row", shifted(0, k + 1)) for k, quarter in enumerate(quarters[1:])]
    part, quarters[0] = lax.optimization_barrier((sum_along(part, True, STEPS), quarters[0]))
    mixed = sum(quarters[1:], quarters[0])
    mixed = sum_along(mixed, True, LARGE_STEPS)
    parts = lax.all_gather(part, "col", axis=0, tiled=True)

    row, col = lax.axis_index("row"), lax.axis_index("col")
    z, c = lax.div(col, 2), lax.rem(col, 2)
    places = [2 * z + c, 2 * z + 1 - c]
    for s in range(1, far):
        for chip in (z + s * (2 * c - 1), z - s * (2 * c - 1)):
            chip = lax.rem(chip + chips, chips)
            places += [2 * chip + c, 2 * chip + 1 - c]
    chip = lax.rem(z + far, chips)
    places += [2 * chip + c, 2 * chip + 1 - c, lax.rem(row, SIDE)]
    places = jnp.stack(places).astype(jnp.int32)

    work, upper = factor_first(parts, width, 2)
    quarters = [mixed] + sent_along(mixed, False, LARGE_STEPS)
    _, _, own_factor, *arranged = factor_second(places, work, upper, 2)
    highs, lows = [high, late_high], [low, late_low]
    top_rows, projected = finish(arranged[:2], arranged[2:], quarters, highs, lows, trailing, 512)
    return (own_factor.T, top_rows, projected)


def solution(mesh):
    placed = (P("row", "col"), P("row", "col"))
    return jax.shard_map(
        on_device,
        mesh=mesh,
        in_specs=placed,
        out_specs=(P(None, "col"), P(None, "col"), P("row", "col")),
        check_vma=False,
    )
```
